32 devices in a mesh: mod: 2 (over y), batch: 16 (over z, x, core).
Axes of the slice: x: 2, y: 2, z: 4, core: 2. Of those that a mesh axis runs over, the one named last changes fastest.
Arguments:
- tokens: bfloat16 [64, 256, 768], P('batch', 'mod'), may hold values from -6 to 6
- caption_lengths: int32 [64], P('batch'), may hold values from 8 to 128, as said below
- region_mask: int32 [64, 128], P('batch'), may hold values from 0 to 1, as said below
- w_qkv: bfloat16 [768, 2304], replicated, may hold values from -0.21875 to 0.21875
- query_bias: float32 [768], replicated, may hold values from -1.5 to 1.5
- value_bias: float32 [768], replicated, may hold values from -1.5 to 1.5
- w_out: bfloat16 [768, 768], replicated, may hold values from -0.875 to 0.875
- out_bias: float32 [768], replicated, may hold values from -1.5 to 1.5
- w_up: bfloat16 [768, 3072], replicated, may hold values from -0.21875 to 0.21875
- up_bias: float32 [3072], replicated, may hold values from -1.5 to 1.5
- w_down: bfloat16 [3072, 768], replicated, may hold values from -0.109375 to 0.109375
- down_bias: float32 [768], replicated, may hold values from -1.5 to 1.5
- gain_one: float32 [768], replicated, may hold values from 0.5 to 1.5
- shift_one: float32 [768], replicated, may hold values from -1.5 to 1.5
- gain_two: float32 [768], replicated, may hold values from 0.5 to 1.5
- shift_two: float32 [768], replicated, may hold values from -1.5 to 1.5
- cotangent: bfloat16 [64, 256, 768], P('batch', 'mod'), may hold values from -6 to 6
Outputs:
- layer_output: bfloat16 [64, 256, 768], P('batch', 'mod')
- input_grad: float32 [64, 256, 768], P('batch', 'mod')
- grad_qkv: float32 [768, 2304], replicated
- grad_query_bias: float32 [768], replicated
- grad_value_bias: float32 [768], replicated
- grad_out: float32 [768, 768], replicated
- grad_out_bias: float32 [768], replicated
- grad_up: float32 [768, 3072], replicated
- grad_up_bias: float32 [3072], replicated
- grad_down: float32 [3072, 768], replicated
- grad_down_bias: float32 [768], replicated
- grad_gain_one: float32 [768], replicated
- grad_shift_one: float32 [768], replicated
- grad_gain_two: float32 [768], replicated
- grad_shift_two: float32 [768], replicated
The draws below stay inside these ranges and needn't reach their ends.
Inputs may be any that keep to these rules, and one draw needn't show every extreme that they name: `caption_lengths`: every caption has 8 to 128 true tokens; some caption has exactly 128 and some exactly 8. `region_mask`: every item has exactly 100 valid regions among its 128 region slots.
All inputs are finite; a program needn't handle non-finite values.
Results may differ from the reference program's by a relative error of at most 0.014.
Values may be sent and summed in bfloat16 or wider, within the bound.
No kernel may reach another device: no remote copies, remote signals or barrier semaphores. Data moves between devices by JAX's collectives and lax.ppermute only.
A program may use at most 192 MiB of HBM per device.

```python
import math
import jax
import jax.numpy as jnp
from jax import lax

D = 768
HEADS = 12
HEAD_DIM = 64
FF = 3072
SLOTS = 128
VALID = 100
MIN_LEN = 8
ITEMS = 64


def draw_caption_lengths(key, part):
    key = jax.random.fold_in(key, 11)
    base_key, long_key, short_key = jax.random.split(key, 3)
    lengths = jax.random.randint(base_key, (ITEMS,), MIN_LEN, SLOTS + 1)
    longest = jax.random.randint(long_key, (), 0, ITEMS)
    shortest = (longest + 1 + jax.random.randint(short_key, (), 0, ITEMS - 1)) % ITEMS
    lengths = lengths.at[longest].set(SLOTS).at[shortest].set(MIN_LEN)
    return lengths.astype(jnp.int32)


def draw_region_mask(key, part):
    key = jax.random.fold_in(key, 23)
    weights_int = jax.random.randint(key, (ITEMS, SLOTS), 0, 1 << 20)
    distinct = weights_int * SLOTS + jnp.arange(SLOTS, dtype=jnp.int32)[None, :]
    order = jnp.argsort(distinct, axis=1)
    ranks = jnp.argsort(order, axis=1)
    return (ranks < VALID).astype(jnp.int32)


def levels(stream_key, dims, shards, least, high):
    loudness = 1.0
    for dim, blocks in shards:
        heights = jax.random.uniform(jax.random.fold_in(jax.random.fold_in(stream_key, 6), dim), (blocks,), jnp.float32, least / len(shards), high / len(shards))
        loudness = loudness * jnp.repeat(jnp.exp(heights), dims[dim] // blocks).reshape((-1,) + (1,) * (len(dims) - 1 - dim))
    return loudness


def bell_draw(own_key, shape, scale, bound, cuts=(), held_as=jnp.bfloat16):
    level = levels(own_key, shape, cuts, -0.22, 0.18) if cuts else 1.0
    values = jax.random.normal(own_key, shape, jnp.float32) * scale * level
    return jnp.minimum(jnp.maximum(values, -bound), bound).astype(held_as)


def setup_inputs(seed: int = 0) -> dict:
    streams_of = jax.random.split(jax.random.key(seed), 18)
    return {
        "tokens": bell_draw(streams_of[0], (ITEMS, 2 * SLOTS, D), 1.0, 6.0, ((0, 16), (1, 2))),
        "caption_lengths": draw_caption_lengths(jax.random.fold_in(streams_of[17], 71), 0),
        "region_mask": draw_region_mask(jax.random.fold_in(streams_of[17], 71), 0),
        "w_qkv": bell_draw(streams_of[3], (D, 3 * D), D ** -0.5, 0.21875),
        "query_bias": bell_draw(streams_of[4], (D,), 0.3, 1.5, (), jnp.float32),
        "value_bias": bell_draw(streams_of[5], (D,), 0.3, 1.5, (), jnp.float32),
        "w_out": bell_draw(streams_of[6], (D, D), (8 * D // SLOTS) ** -0.5, 0.875),
        "out_bias": bell_draw(streams_of[7], (D,), 0.3, 1.5, (), jnp.float32),
        "w_up": bell_draw(streams_of[8], (D, FF), D ** -0.5, 0.21875),
        "up_bias": bell_draw(streams_of[9], (FF,), 0.3, 1.5, (), jnp.float32),
        "w_down": bell_draw(streams_of[10], (FF, D), FF ** -0.5, 0.109375),
        "down_bias": bell_draw(streams_of[11], (D,), 0.3, 1.5, (), jnp.float32),
        "gain_one": jnp.clip(1.0 + 0.1 * jax.random.normal(streams_of[12], (D,), jnp.float32), 0.5, 1.5),
        "shift_one": bell_draw(streams_of[13], (D,), 0.3, 1.5, (), jnp.float32),
        "gain_two": jnp.clip(1.0 + 0.1 * jax.random.normal(streams_of[14], (D,), jnp.float32), 0.5, 1.5),
        "shift_two": bell_draw(streams_of[15], (D,), 0.3, 1.5, (), jnp.float32),
        "cotangent": bell_draw(streams_of[16], (ITEMS, 2 * SLOTS, D), 1.0, 6.0, ((0, 16), (1, 2))),
    }


@jax.custom_vjp
def low(v):
    return lax.optimization_barrier(v.astype(jnp.bfloat16)).astype(jnp.float32)

@jax.custom_vjp
def low_back(v):
    return v

def low_keep(v):
    return (low(v), None)

def low_pass(kept, grad):
    return (grad,)

def back_keep(v):
    return (v, None)

def back_low(kept, grad):
    return (low(grad),)
low.defvjp(low_keep, low_pass)
low_back.defvjp(back_keep, back_low)

def product(left, right):
    return jnp.dot(left, right, precision=lax.Precision.HIGHEST)

def layer_norm(values_in, gain, shift):
    center = lax.optimization_barrier(jnp.mean(values_in, axis=-1, keepdims=True))
    centered = values_in - center
    variance = lax.optimization_barrier(jnp.mean(centered * centered, axis=-1, keepdims=True))
    return centered * lax.rsqrt(variance + 1e-12) * gain + shift

def forward(params, inputs, key_valid):
    w_qkv, query_bias, value_bias, w_out, out_bias, w_up, up_bias, w_down, down_bias, gain_one, shift_one, gain_two, shift_two = params
    group, length, width = inputs.shape
    flat = inputs.reshape(group * length, width)
    joined = product(flat, w_qkv)
    shaped = (group, length, HEADS, HEAD_DIM)
    queries = low_back(low(joined[:, :width] + query_bias)).reshape(shaped)
    keys = low_back(low(joined[:, width:2 * width])).reshape(shaped)
    values = low_back(low(joined[:, 2 * width:] + value_bias)).reshape(shaped)
    scale = HEAD_DIM ** (-0.5)
    scores = jnp.einsum('ishd,ijhd->ihsj', queries, keys, precision=lax.Precision.HIGHEST) * scale
    scores = jnp.where(key_valid[:, None, None, :], scores, -1e+30)
    scores = low_back(scores)
    probs = jax.nn.softmax(scores, axis=-1)
    attended = jnp.einsum('ihsj,ijhd->ishd', low(probs), values, precision=lax.Precision.HIGHEST)
    attended = low_back(low(attended.reshape(group * length, width)))
    branch = low_back(product(attended, w_out) + out_bias)
    normed = layer_norm(flat + branch, gain_one, shift_one)
    upward = low_back(product(low(normed), w_up) + up_bias)
    activated = low(jax.nn.gelu(upward, approximate=False))
    down_branch = low_back(product(activated, w_down) + down_bias)
    result = layer_norm(normed + down_branch, gain_two, shift_two)
    return result.reshape(group, length, width)

def reference(tokens, caption_lengths, region_mask, w_qkv, query_bias, value_bias, w_out, out_bias, w_up, up_bias, w_down, down_bias, gain_one, shift_one, gain_two, shift_two, cotangent):
    item_count = tokens.shape[0]
    group = math.gcd(item_count, 16)
    blocks_count = item_count // group
    params = tuple((weight.astype(jnp.float32) for weight in (w_qkv, query_bias, value_bias, w_out, out_bias, w_up, up_bias, w_down, down_bias, gain_one, shift_one, gain_two, shift_two)))
    slot_index = jnp.arange(SLOTS, dtype=jnp.int32)
    text_valid = slot_index[None, :] < caption_lengths[:, None]
    key_valid = jnp.concatenate([text_valid, region_mask > 0], axis=1)
    length = tokens.shape[1]
    width = tokens.shape[2]
    token_blocks = tokens.reshape(blocks_count, group, length, width)
    valid_blocks = key_valid.reshape(blocks_count, group, length)
    cot_blocks = cotangent.reshape(blocks_count, group, length, width)

    def step(totals, block):
        inputs, valid, cot = block

        def apply_layer(weights_in, rows_in):
            return forward(weights_in, rows_in, valid)
        result, pullback = jax.vjp(apply_layer, params, inputs.astype(jnp.float32))
        grad_params, grad_inputs = pullback(cot.astype(jnp.float32))
        totals = jax.tree.map(jnp.add, totals, grad_params)
        return (totals, (result.astype(jnp.bfloat16), grad_inputs))
    starting = jax.tree.map(jnp.zeros_like, params)
    totals, (outputs, input_grads) = lax.scan(step, starting, (token_blocks, valid_blocks, cot_blocks))
    layer_output = outputs.reshape(item_count, length, width)
    input_grad = input_grads.reshape(item_count, length, width)
    return (layer_output, input_grad, totals[0], totals[1], totals[2], totals[3], totals[4], totals[5], totals[6], totals[7], totals[8], totals[9], totals[10], totals[11], totals[12])
```

```python
import functools

import jax
import jax.numpy as jnp
from jax import lax
from jax.experimental import pallas as pl
from jax.experimental.pallas import tpu as pltpu
from jax.sharding import PartitionSpec as P

HEADS = 12
HEAD_DIM = 64
WIDTH = 768
FF = 3072
SLOTS = 128
EPSILON = 1e-12
PAIR = 2 * HEAD_DIM
HALF = WIDTH // 2
FF_HALF = FF // 2
CHUNK = 512
CHUNKS = FF // CHUNK
MASKED = -1e30
SCALE = HEAD_DIM ** (-0.5)
MIB = 1 << 20

BF16 = jnp.bfloat16
F32 = jnp.float32


def nn(left, right):
    return lax.dot_general(left, right, (((1,), (0,)), ((), ())), preferred_element_type=F32)


def nt(left, right):
    return lax.dot_general(left, right, (((1,), (1,)), ((), ())), preferred_element_type=F32)


def tn(left, right):
    return lax.dot_general(left, right, (((0,), (0,)), ((), ())), preferred_element_type=F32)


def whole(shape):
    zeros = (0,) * len(shape)
    return pl.BlockSpec(shape, lambda *_: zeros, pipeline_mode=pl.Buffered(1))


TOKEN = (8, 128)
RATE = 10e9


def run(body, name, pos, grid, inputs, outputs, us, mib, after=(), scratch=()):
    tokens = len(after)
    first = 1 + len(inputs)
    last = first + tokens + len(outputs)

    def wrapped(*refs):
        refs[last][...] = jnp.zeros(TOKEN, F32)
        body(*refs[:first], *refs[first + tokens : last], *refs[last + 1 :])

    out = pl.pallas_call(
        wrapped,
        grid_spec=pltpu.PrefetchScalarGridSpec(
            num_scalar_prefetch=1,
            grid=grid,
            in_specs=[spec for _, spec in inputs]
            + [pl.BlockSpec(memory_space=pl.ANY)] * tokens,
            out_specs=[spec for _, _, spec in outputs] + [whole(TOKEN)],
            scratch_shapes=list(scratch),
        ),
        out_shape=[jax.ShapeDtypeStruct(shape, kind) for shape, kind, _ in outputs]
        + [jax.ShapeDtypeStruct(TOKEN, F32)],
        compiler_params=pltpu.CompilerParams(
            dimension_semantics=("arbitrary",) * len(grid), vmem_limit_bytes=mib * MIB
        ),
        cost_estimate=pl.CostEstimate(flops=int(us * RATE), bytes_accessed=1000, transcendentals=0),
        name=name,
    )(pos, *[array for array, _ in inputs], *after)
    return out[:-1], out[-1]


def lane_half(shape):
    return lax.broadcasted_iota(jnp.int32, shape, 1) >= HEAD_DIM


def head_operands(upper, head, query, key, ones, mask):
    if head == 0:
        return jnp.where(upper, ones, query), jnp.where(upper, mask, key)
    return jnp.where(upper, query, ones), jnp.where(upper, key, mask)


def softmax_over_keys(scores):
    exponent = jnp.exp(scores - jnp.max(scores, axis=0, keepdims=True))
    return exponent * (1.0 / jnp.sum(exponent, axis=0, keepdims=True))


def norm(rows):
    center = jnp.mean(rows, axis=-1, keepdims=True)
    centered = rows - center
    variance = jnp.mean(centered * centered, axis=-1, keepdims=True)
    inverse = lax.rsqrt(variance + EPSILON)
    return centered * inverse, inverse


def norm_back(grad_result, scaled, inverse, gain):
    grad_scaled = grad_result * gain
    first_mean = jnp.mean(grad_scaled, axis=-1, keepdims=True)
    second_mean = jnp.mean(grad_scaled * scaled, axis=-1, keepdims=True)
    return inverse * (grad_scaled - first_mean - scaled * second_mean)


GROUP = 256
GROUPS = WIDTH // GROUP


def attend_body(
    items,
    pos,
    own,
    other,
    mask,
    ones,
    w_q,
    w_k,
    w_v,
    query_bias,
    value_bias,
    w_out,
    out_bias,
    gain,
    shift,
    queries,
    keys,
    values,
    keep,
    normed,
    scaled,
    inverse,
    total,
    attended,
):
    step = pl.program_id(0)
    span = 2 * SLOTS
    rows_out = keep.at[0]

    @pl.when(step == 0)
    def _():
        for item in range(items):
            rows_out[item * span : item * span + SLOTS, :] = own[item]
            rows_out[item * span + SLOTS : (item + 1) * span, :] = other[item]
        total[...] = jnp.zeros_like(total)

    rows = rows_out[...]
    queries[...] = (nn(rows, w_q[...]) + query_bias[...]).astype(BF16)
    keys[...] = nn(rows, w_k[...]).astype(BF16)
    values[...] = (nn(rows, w_v[...]) + value_bias[...]).astype(BF16)
    upper = lane_half((span, PAIR))
    for item in range(items):
        at = slice(item * span, (item + 1) * span)
        for pair in range(GROUP // PAIR):
            cols = slice(pair * PAIR, (pair + 1) * PAIR)
            query = queries[at, cols] * jnp.asarray(SCALE, BF16)
            key = keys[at, cols]
            value = values[at, cols]
            parts = []
            for head in range(2):
                query_h, key_h = head_operands(
                    upper, head, query, key, ones[...], mask[item]
                )
                probs = softmax_over_keys(nt(key_h, query_h))
                parts.append(tn(probs.astype(BF16), value))
            attended[at, cols] = jnp.where(upper, parts[1], parts[0]).astype(BF16)
    total[...] += nn(attended[...], w_out[...])
    keep[1, :, pl.ds(pl.multiple_of(step * GROUP, GROUP), GROUP)] = attended[...]

    @pl.when(step == GROUPS - 1)
    def _():
        summed = rows_out[...].astype(F32) + (total[...] + out_bias[...])
        unit, inv = norm(summed)
        result = unit * gain[...] + shift[...]
        scaled[...] = unit
        inverse[...] = inv
        normed[...] = result
        keep[2] = result.astype(BF16)


def attend(pos, own, other, mask, ones, w_qkv, query_bias, value_bias, w_out, out_bias, gain, shift):
    items = own.shape[0]
    count = items * 2 * SLOTS
    row = pl.BlockSpec((1, GROUP), lambda g, pos: (0, g))
    flat = pl.BlockSpec((count, GROUP), lambda g, pos: (0, g))
    full = whole((count, WIDTH))
    vector = whole((1, WIDTH))
    weight = lambda k: pl.BlockSpec((WIDTH, GROUP), lambda g, pos: (0, k * GROUPS + g))
    shape = (count, WIDTH)
    return run(
        functools.partial(attend_body, items),
        "attend",
        pos,
        (GROUPS,),
        [
            (own, whole(own.shape)),
            (other, whole(other.shape)),
            (mask, whole(mask.shape)),
            (ones, whole(ones.shape)),
            (w_qkv, weight(0)),
            (w_qkv, weight(1)),
            (w_qkv, weight(2)),
            (query_bias, row),
            (value_bias, row),
            (w_out, pl.BlockSpec((GROUP, WIDTH), lambda g, pos: (g, 0))),
            (out_bias, vector),
            (gain, vector),
            (shift, vector),
        ],
        [
            (shape, BF16, flat),
            (shape, BF16, flat),
            (shape, BF16, flat),
            ((3,) + shape, BF16, whole((3,) + shape)),
            (shape, F32, full),
            (shape, F32, full),
            ((count, 1), F32, whole((count, 1))),
        ],
        scratch=[pltpu.VMEM(shape, F32), pltpu.VMEM((count, GROUP), BF16)],
        us=8,
        mib=24,
    )


def feed_body(
    items,
    pos,
    normed,
    normed_low,
    w_up,
    up_bias,
    w_down,
    down_bias,
    gain,
    shift,
    cot_own,
    cot_other,
    act_mine,
    slope,
    send,
    out_own,
    out_other,
    grad_second,
    small,
    total,
):
    step = pl.program_id(0)
    span = 2 * SLOTS
    upward = nn(normed_low[...], w_up[...]) + up_bias[...]
    phi = 0.5 + 0.5 * lax.erf(upward * 0.7071067811865476)
    density = jnp.exp(-0.5 * upward * upward) * 0.3989422804014327
    slope[...] = (phi + upward * density).astype(slope.dtype)
    active = (upward * phi).astype(BF16)

    @pl.when(step < CHUNKS // 2)
    def _():
        send[:, pl.ds(pl.multiple_of(step * CHUNK, CHUNK), CHUNK)] = active

    @pl.when(step >= CHUNKS // 2)
    def _():
        act_mine[...] = active

    part = nn(active, w_down[...])

    @pl.when(step == 0)
    def _():
        total[...] = part

    @pl.when(step > 0)
    def _():
        total[...] += part

    @pl.when(step == CHUNKS - 1)
    def _():
        unit, inv = norm(normed[...] + (total[...] + down_bias[...]))
        result = (unit * gain[...] + shift[...]).astype(BF16)
        cots = []
        for item in range(items):
            out_own[item] = result[item * span : item * span + SLOTS]
            out_other[item] = result[item * span + SLOTS : (item + 1) * span]
            cots += [cot_own[item], cot_other[item]]
        cot = jnp.concatenate(cots, axis=0).astype(F32)
        grad = norm_back(cot, unit, inv, gain[...])
        low = grad.astype(BF16)
        grad_second[...] = grad
        send[:, FF_HALF:] = low
        small[0:1, :] = jnp.sum(low.astype(F32), axis=0, keepdims=True)
        small[1:2, :] = jnp.sum(cot * unit, axis=0, keepdims=True)
        small[2:3, :] = jnp.sum(cot, axis=0, keepdims=True)


def half_chunk(j, pos):
    return lax.rem(j + (1 - pos[0]) * (CHUNKS // 2), CHUNKS)


def keep_rows(which, count, cols, place):
    return pl.BlockSpec((None, count, cols), lambda j, pos: (which, 0, place(j, pos)))


def feed(pos, normed, keep, w_up, up_bias, w_down, down_bias, gain, shift, cot_own, cot_other):
    count = normed.shape[0]
    items = cot_own.shape[0]
    full = whole((count, WIDTH))
    vector = whole((1, WIDTH))
    rows = whole(cot_own.shape)
    half = CHUNKS // 2
    return run(
        functools.partial(feed_body, items),
        "feed",
        pos,
        (CHUNKS,),
        [
            (normed, full),
            (keep, keep_rows(2, count, WIDTH, lambda j, pos: 0)),
            (w_up, pl.BlockSpec((WIDTH, CHUNK), lambda j, pos: (0, half_chunk(j, pos)))),
            (up_bias, pl.BlockSpec((1, CHUNK), lambda j, pos: (0, half_chunk(j, pos)))),
            (w_down, pl.BlockSpec((CHUNK, WIDTH), lambda j, pos: (half_chunk(j, pos), 0))),
            (down_bias, vector),
            (gain, vector),
            (shift, vector),
            (cot_own, rows),
            (cot_other, rows),
        ],
        [
            (
                (count, FF_HALF),
                BF16,
                pl.BlockSpec((count, CHUNK), lambda j, pos: (0, jnp.maximum(j - half, 0))),
            ),
            ((count, FF), F32, pl.BlockSpec((count, CHUNK), lambda j, pos: (0, j))),
            ((count, FF_HALF + WIDTH), BF16, whole((count, FF_HALF + WIDTH))),
            (cot_own.shape, BF16, rows),
            (cot_own.shape, BF16, rows),
            ((count, WIDTH), F32, full),
            ((8, WIDTH), F32, whole((8, WIDTH))),
        ],
        scratch=[pltpu.VMEM((count, WIDTH), F32)],
        us=10,
        mib=28,
    )


def hidden_back(grad_low, slope, w_down, w_up, up_grad, up_bias_grad, total, before=None):
    low = (nt(grad_low[...], w_down[...]) * slope[...].astype(F32)).astype(BF16)
    up_grad[...] = low
    up_bias_grad[...] = jnp.sum(low.astype(F32), axis=0, keepdims=True)
    part = nt(low, w_up[...])

    @pl.when(pl.program_id(0) == 0)
    def _():
        total[...] = part if before is None else part + before[...]

    @pl.when(pl.program_id(0) > 0)
    def _():
        total[...] += part


def feed_back_first(pos, grad_low, slope, w_down, w_up, up_grad, up_bias_grad, total):
    hidden_back(grad_low, slope, w_down, w_up, up_grad, up_bias_grad, total)


def feed_back_second(
    pos,
    grad_low,
    slope,
    w_down,
    w_up,
    before,
    grad_second,
    scaled,
    inverse,
    gain,
    w_out,
    up_grad,
    up_bias_grad,
    grad_first,
    branch_theirs,
    branch_mine,
    grad_attended,
    small,
    total,
    branch,
):
    hidden_back(grad_low, slope, w_down, w_up, up_grad, up_bias_grad, total, before)

    @pl.when(pl.program_id(0) == CHUNKS // 2 - 1)
    def _():
        grad_normed = total[...] + grad_second[...]
        unit = scaled[...]
        grad = norm_back(grad_normed, unit, inverse[...], gain[...])
        grad_first[...] = grad
        branch[...] = grad.astype(BF16)
        mine = pl.multiple_of(pos[0] * HALF, HALF)
        theirs = pl.multiple_of((1 - pos[0]) * HALF, HALF)
        branch_mine[...] = branch[:, pl.ds(mine, HALF)]
        branch_theirs[...] = branch[:, pl.ds(theirs, HALF)]
        grad_attended[...] = nt(branch[...], w_out[...]).astype(BF16)
        small[0:1, :] = jnp.sum(branch[...].astype(F32), axis=0, keepdims=True)
        small[1:2, :] = jnp.sum(grad_normed * unit, axis=0, keepdims=True)
        small[2:3, :] = jnp.sum(grad_normed, axis=0, keepdims=True)


def feed_back(first, pos, send, slope, w_down, w_up, more, after):
    count = send.shape[0]
    full = whole((count, WIDTH))
    narrow = whole((count, HALF))
    steps = CHUNKS // 2
    start = 0 if first else steps
    real = lambda j, pos: half_chunk(j + start, pos)
    hidden = pl.BlockSpec((count, CHUNK), lambda j, pos: (0, j))
    inputs = [
        (send, pl.BlockSpec((count, WIDTH), lambda j, pos: (0, FF_HALF // WIDTH))),
        (slope, pl.BlockSpec((count, CHUNK), lambda j, pos: (0, j + start))),
        (w_down, pl.BlockSpec((CHUNK, WIDTH), lambda j, pos: (real(j, pos), 0))),
        (w_up, pl.BlockSpec((WIDTH, CHUNK), lambda j, pos: (0, real(j, pos)))),
    ] + [(a, whole(a.shape)) for a in more]
    outputs = [
        ((count, FF_HALF), BF16, hidden),
        ((1, FF_HALF), F32, pl.BlockSpec((1, CHUNK), lambda j, pos: (0, j))),
        ((count, WIDTH), F32, full),
    ]
    scratch = []
    if not first:
        outputs += [
            ((count, HALF), BF16, narrow),
            ((count, HALF), BF16, narrow),
            ((count, WIDTH), BF16, full),
            ((8, WIDTH), F32, whole((8, WIDTH))),
        ]
        scratch = [pltpu.VMEM((count, WIDTH), F32), pltpu.VMEM((count, WIDTH), BF16)]
    return run(
        feed_back_first if first else feed_back_second,
        "feed_back_first" if first else "feed_back_second",
        pos,
        (steps,),
        inputs,
        outputs,
        after=after,
        scratch=scratch,
        us=6,
        mib=30,
    )


def attend_back_half(
    items, mask, ones, queries, keys, values, grad_attended, w_q, w_k, w_v, branch, joined
):
    span = 2 * SLOTS
    upper = lane_half((span, PAIR))
    for item in range(items):
        at = slice(item * span, (item + 1) * span)
        for pair in range(HALF // PAIR):
            cols = slice(pair * PAIR, (pair + 1) * PAIR)
            query = queries[at, cols] * jnp.asarray(SCALE, BF16)
            key = keys[at, cols]
            value = values[at, cols]
            grad_out = grad_attended[at, cols]
            none = jnp.zeros_like(grad_out)
            grads = []
            for head in range(2):
                query_h, key_h = head_operands(
                    upper, head, query, key, ones[...], mask[item]
                )
                probs = softmax_over_keys(nt(key_h, query_h))
                if head == 0:
                    grad_h = jnp.where(upper, none, grad_out)
                else:
                    grad_h = jnp.where(upper, grad_out, none)
                grad_probs = nt(value, grad_h)
                inner = jnp.sum(probs * grad_probs, axis=0, keepdims=True)
                grad_scores = (probs * (grad_probs - inner)).astype(BF16)
                grads.append(
                    (
                        tn(grad_scores, key) * SCALE,
                        nn(grad_scores, query),
                        nn(probs.astype(BF16), grad_out),
                    )
                )
            for index in range(3):
                place = slice(index * HALF + pair * PAIR, index * HALF + (pair + 1) * PAIR)
                joined[at, place] = jnp.where(
                    upper, grads[1][index], grads[0][index]
                ).astype(BF16)
    joined[:, 3 * HALF :] = branch[...]
    parts = [joined[:, index * HALF : (index + 1) * HALF] for index in range(3)]
    sums = [jnp.sum(parts[index].astype(F32), axis=0, keepdims=True) for index in (0, 2)]
    total = nt(parts[0], w_q[...]) + nt(parts[1], w_k[...]) + nt(parts[2], w_v[...])
    return total, sums


def attend_back_first(items, pos, *refs):
    *ins, grad_first, joined, total, bias = refs
    part, sums = attend_back_half(items, *ins, joined)
    total[...] = grad_first[...] + part
    for index in range(2):
        bias[index : index + 1, :] = sums[index]


def attend_back_second(items, pos, *refs):
    *ins, before, before_bias, small_one, small_two, up_theirs, up_mine, joined, own, other, small = refs
    span = 2 * SLOTS
    part, sums = attend_back_half(items, *ins, joined)
    for item in range(items):
        at = item * span
        own[item] = before[at : at + SLOTS, :] + part[at : at + SLOTS]
        other[item] = (before[at + SLOTS : at + span, :] + part[at + SLOTS : at + span]).astype(BF16)
    mine = pl.multiple_of(pos[0] * HALF, HALF)
    theirs = pl.multiple_of((1 - pos[0]) * HALF, HALF)
    small[...] = jnp.zeros_like(small)
    small[0:3, :] = small_one[0:3, :]
    small[3:6, :] = small_two[0:3, :]
    for index in range(2):
        cols = slice(index * WIDTH, (index + 1) * WIDTH)
        small[pl.ds(6 + 2 * pos[0] + index, 1), :] = up_mine[:, cols]
        small[pl.ds(8 - 2 * pos[0] + index, 1), :] = up_theirs[:, cols]
    for index in range(2):
        small[10 + index : 11 + index, pl.ds(mine, HALF)] = sums[index]
        small[10 + index : 11 + index, pl.ds(theirs, HALF)] = before_bias[index : index + 1, :]


def attend_back(first, pos, mask, ones, queries, keys, values, grad_attended, w_qkv, branch, more, after):
    count = queries.shape[0]
    items = mask.shape[0]
    half = (lambda pos: 1 - pos[0]) if first else (lambda pos: pos[0])
    flat = pl.BlockSpec((count, HALF), lambda j, pos: (0, half(pos)))
    weight = lambda k: pl.BlockSpec((WIDTH, HALF), lambda j, pos: (0, 2 * k + half(pos)))
    joined = ((count, 4 * HALF), BF16, whole((count, 4 * HALF)))
    rows = whole((items, SLOTS, WIDTH))
    if first:
        outputs = [
            joined,
            ((count, WIDTH), F32, whole((count, WIDTH))),
            ((8, HALF), F32, whole((8, HALF))),
        ]
    else:
        outputs = [
            joined,
            ((items, SLOTS, WIDTH), F32, rows),
            ((items, SLOTS, WIDTH), BF16, rows),
            ((16, WIDTH), F32, whole((16, WIDTH))),
        ]
    return run(
        functools.partial(attend_back_first if first else attend_back_second, items),
        "attend_back_first" if first else "attend_back_second",
        pos,
        (1,),
        [
            (mask, whole(mask.shape)),
            (ones, whole(ones.shape)),
            (queries, flat),
            (keys, flat),
            (values, flat),
            (grad_attended, flat),
            (w_qkv, weight(0)),
            (w_qkv, weight(1)),
            (w_qkv, weight(2)),
            (branch, whole(branch.shape)),
        ]
        + [(a, whole(a.shape)) for a in more],
        outputs,
        after=after,
        us=6,
        mib=18,
    )


TALL = HALF
LOW = TALL // 2
SHARE = TALL // 4
SHARES = (SHARE,) * 4


def quarter(pos, there):
    across = pos[1] if there < 2 else 1 - pos[1]
    along = pos[2] if there % 2 == 0 else 1 - pos[2]
    return across, along


def gradient_body(size, block, plan, pos, *refs):
    scratch = 1 if any(cuts == SHARES for _, _, cuts in plan) else 0
    last = len(refs) - scratch
    first = last - sum(len(cuts) for _, _, cuts in plan)
    outs = refs[first:last]
    extra = refs[size * len(plan) : first]
    at = 0
    for index, (there, adds, cuts) in enumerate(plan):
        value = block(there, pos, *refs[index * size : (index + 1) * size])
        for number, start in adds:
            more = extra[number][...].astype(F32)
            rows = more.shape[0]
            if rows == TALL:
                value = value + more
            elif start == 0:
                value = jnp.concatenate([value[:rows] + more, value[rows:]], axis=0)
            else:
                value = jnp.concatenate([value[:start], value[start:] + more], axis=0)
        if cuts == SHARES:
            held = refs[-1]
            held[...] = value
            for turn in range(4):
                first = pl.multiple_of((pos[3] ^ turn) * SHARE, SHARE)
                outs[at][...] = held[pl.ds(first, SHARE), :].astype(BF16)
                at += 1
            continue
        start = 0
        for cut in cuts:
            outs[at][...] = value[start : start + cut].astype(BF16)
            start += cut
            at += 1


def plain_block(there, pos, left_a, left_b, right_a, right_b):
    return tn(left_a[...], right_a[...]) + tn(left_b[...], right_b[...])


def mixed_block(there, pos, rows_a, rows_b, att_a, att_b, right_a, right_b):
    along = quarter(pos, there)[1] == 0
    left_a = jnp.where(along, rows_a[...], att_a[...])
    left_b = jnp.where(along, rows_b[...], att_b[...])
    return jnp.concatenate(
        [
            tn(rows_a[...], right_a[:, :HALF]) + tn(rows_b[...], right_b[:, :HALF]),
            tn(left_a, right_a[:, HALF:]) + tn(left_b, right_b[:, HALF:]),
        ],
        axis=1,
    )


def up_specs(there, count):
    lefts = keep_rows(2, count, TALL, lambda j, pos: quarter(pos, there)[0])
    rights = pl.BlockSpec((count, WIDTH), lambda j, pos: (0, quarter(pos, there)[1]))
    return [lefts, lefts, rights, rights]


def mixed_specs(there, count):
    rows = keep_rows(0, count, TALL, lambda j, pos: quarter(pos, there)[0])
    att = keep_rows(1, count, TALL, lambda j, pos: quarter(pos, there)[0])
    rights = pl.BlockSpec((count, WIDTH), lambda j, pos: (0, quarter(pos, there)[1]))
    return [rows, rows, att, att, rights, rights]


KINDS = {
    "up": (plain_block, up_specs),
    "mixed": (mixed_block, mixed_specs),
}


def gradient(kind, pos, operands, plan, after, extra=()):
    block, specs = KINDS[kind]
    count = operands[-1].shape[0]
    inputs = []
    for there, _, _ in plan:
        inputs += list(zip(operands, specs(there, count)))
    return run(
        functools.partial(gradient_body, len(operands), block, plan),
        kind + "_grad_" + "".join(str(there) for there, _, _ in plan),
        pos,
        (1,),
        inputs + [(e, whole(e.shape)) for e in extra],
        [((cut, WIDTH), BF16, whole((cut, WIDTH))) for _, _, cuts in plan for cut in cuts],
        after=after,
        scratch=[pltpu.VMEM((TALL, WIDTH), F32) for _, _, cuts in plan if cuts == SHARES],
        us=1,
        mib=14,
    )


def down_body(pos, left_a, left_b, right_a, right_b, out):
    out[...] = (tn(left_a[...], right_a[...]) + tn(left_b[...], right_b[...])).astype(BF16)


def down_gradient(pos, operands, after):
    count = operands[0].shape[0]
    lefts = pl.BlockSpec((count, TALL), lambda j, pos: (0, j))
    rights = pl.BlockSpec((count, WIDTH), lambda j, pos: (0, FF_HALF // WIDTH))
    out, token = run(
        down_body,
        "down_grad",
        pos,
        (FF_HALF // TALL,),
        list(zip(operands, [lefts, lefts, rights, rights])),
        [((FF_HALF, WIDTH), BF16, pl.BlockSpec((TALL, WIDTH), lambda j, pos: (j, 0)))],
        after=after,
        us=3,
        mib=14,
    )
    return out[0], token


def add_body(pos, *refs):
    total = refs[0][...].astype(F32)
    for ref in refs[1:-1]:
        total = total + ref[...].astype(F32)
    refs[-1][...] = total.astype(BF16)


def sum_of(pos, shares, after):
    shape = shares[0].shape
    out, token = run(
        add_body,
        "sum_of",
        pos,
        (1,),
        [(a, whole(shape)) for a in shares],
        [(shape, BF16, whole(shape))],
        after=after,
        us=1,
        mib=4,
    )
    return out[0], token


def join_body(pos, *refs):
    for turn in range(4):
        first = pl.multiple_of((pos[3] ^ turn) * SHARE, SHARE)
        refs[-1][pl.ds(first, SHARE), :] = refs[turn][...]


def join_shares(pos, shares, after):
    shape = (TALL, WIDTH)
    out, token = run(
        join_body,
        "join_shares",
        pos,
        (1,),
        [(a, whole(a.shape)) for a in shares],
        [(shape, BF16, whole(shape))],
        after=after,
        us=1,
        mib=6,
    )
    return out[0], token


def read_piece(pieces, step):
    each = len(pieces) // 2
    own, along, across, *last = pieces[each * (step // 4) : each * (step // 4 + 1)]
    kind = step % 4
    if kind == 3:
        return jnp.concatenate([part[...] for part in last], axis=0).astype(F32)
    return (own, along, across)[kind][...].astype(F32)


def piece_place(step, pos):
    half = jnp.where(step < 4, pos[0], 1 - pos[0])
    kind = lax.rem(step, 4)
    along = jnp.where(lax.rem(kind, 2) == 0, pos[2], 1 - pos[2])
    across = jnp.where(kind < 2, pos[1], 1 - pos[1])
    return half, across, along


def place_body(pos, *refs):
    out = refs[-1]
    step = pl.program_id(0)
    for index in range(8):

        @pl.when(step == index)
        def _(index=index):
            out[...] = read_piece(refs[:-1], index)


def place_mixed_body(pos, *refs):
    joint, branch = refs[-2:]
    step = pl.program_id(0)
    part = pl.program_id(1)
    along = piece_place(step, pos)[2]
    for index in range(8):

        @pl.when((step == index) & (part == 0))
        def _(index=index):
            joint[...] = read_piece(refs[:-2], index)[:, :HALF]

        @pl.when((step == index) & (part == 1) & (along == 0))
        def _(index=index):
            joint[...] = read_piece(refs[:-2], index)[:, HALF:]

        @pl.when((step == index) & (part == 1) & (along == 1))
        def _(index=index):
            branch[...] = read_piece(refs[:-2], index)[:, HALF:]


def place(pos, pieces, after):
    def where(step, pos):
        half, across, along = piece_place(step, pos)
        return (across, 2 * half + along)

    out, token = run(
        place_body,
        "place",
        pos,
        (8,),
        [(piece, whole(piece.shape)) for piece in pieces],
        [((WIDTH, FF), F32, pl.BlockSpec((TALL, WIDTH), where))],
        after=after,
        us=4,
        mib=14,
    )
    return out[0], token


def place_down_body(pos, mine, theirs, out):
    step = pl.program_id(0)
    half = FF_HALF // TALL

    @pl.when(step < half)
    def _():
        out[...] = mine[...].astype(F32)

    @pl.when(step >= half)
    def _():
        out[...] = theirs[...].astype(F32)


def place_down(pos, mine, theirs, after):
    half = FF_HALF // TALL

    def where(step, pos):
        return (lax.rem(step + half * pos[0], 2 * half), 0)

    out, token = run(
        place_down_body,
        "place_down",
        pos,
        (2 * half,),
        [
            (mine, pl.BlockSpec((TALL, WIDTH), lambda j, pos: (jnp.minimum(j, half - 1), 0))),
            (theirs, pl.BlockSpec((TALL, WIDTH), lambda j, pos: (jnp.maximum(j - half, 0), 0))),
        ],
        [((FF, WIDTH), F32, pl.BlockSpec((TALL, WIDTH), where))],
        after=after,
        us=4,
        mib=14,
    )
    return out[0], token


def place_mixed(pos, pieces, after):
    def joint(step, part, pos):
        half, across, along = piece_place(step, pos)
        column = jnp.minimum(2 * along + part, 2)
        return (across, 2 * column + half)

    def branch(step, part, pos):
        half, across, _ = piece_place(step, pos)
        return (across, half)

    return run(
        place_mixed_body,
        "place_mixed",
        pos,
        (8, 2),
        [(piece, whole(piece.shape)) for piece in pieces],
        [
            ((WIDTH, 3 * WIDTH), F32, pl.BlockSpec((TALL, HALF), joint)),
            ((WIDTH, WIDTH), F32, pl.BlockSpec((TALL, HALF), branch)),
        ],
        after=after,
        us=4,
        mib=14,
    )


def place_rows_body(pos, own, got, own_grad, got_grad, out, grad):
    @pl.when(pl.program_id(0) == 0)
    def _():
        out[...] = own[...]
        grad[...] = own_grad[...]

    @pl.when(pl.program_id(0) == 1)
    def _():
        out[...] = got[...]
        grad[...] = got_grad[...].astype(F32)


def place_rows(pos, own, got, own_grad, got_grad, after):
    items = own.shape[0]
    spec = pl.BlockSpec(
        own.shape, lambda step, pos: (jnp.where(step == 0, pos[1], 1 - pos[1]), 0, 0)
    )
    shape = (2 * items,) + own.shape[1:]
    return run(
        place_rows_body,
        "place_rows",
        pos,
        (2,),
        [(a, whole(own.shape)) for a in (own, got, own_grad, got_grad)],
        [(shape, BF16, spec), (shape, F32, spec)],
        after=after,
        us=2,
        mib=10,
    )


def local(
    batch,
    tokens,
    caption_lengths,
    region_mask,
    w_qkv,
    query_bias,
    value_bias,
    w_out,
    out_bias,
    w_up,
    up_bias,
    w_down,
    down_bias,
    gain_one,
    shift_one,
    gain_two,
    shift_two,
    cotangent,
):
    swap_core = [(i, i ^ 1) for i in range(batch)]
    swap_along = [(i, i ^ 2) for i in range(batch)]
    swap_across = [(0, 1), (1, 0)]
    line = [[4 * k + i for k in range(batch // 4)] for i in range(4)]
    same_core = [[2 * k + i for k in range(batch // 2)] for i in range(2)]
    core = lambda a: lax.ppermute(a, "batch", swap_core)
    along = lambda a: lax.ppermute(a, "batch", swap_along)
    across = lambda a: lax.ppermute(a, "mod", swap_across)

    place_y = lax.axis_index("mod")
    place_b = lax.axis_index("batch")
    pos = jnp.stack([place_b % 2, place_y, (place_b // 2) % 2, (place_b // 4) % 4]).astype(jnp.int32)
    items = tokens.shape[0] // 2
    mine = place_y * items
    rest = (1 - place_y) * items
    rows = lambda a, start: lax.dynamic_slice_in_dim(a, start, items, axis=0)

    other_tokens = across(rows(tokens, rest))
    other_cot = across(rows(cotangent, rest))
    own_tokens = rows(tokens, mine)
    own_cot = rows(cotangent, mine)

    slot = lax.broadcasted_iota(jnp.int32, (items, SLOTS), 1)
    text = slot < rows(caption_lengths, mine)[:, None]
    region = rows(region_mask, mine) > 0
    valid = jnp.concatenate(
        [jnp.where(place_y == 0, text, region), jnp.where(place_y == 0, region, text)], axis=1
    )
    lane = lax.broadcasted_iota(jnp.int32, (1, 1, PAIR), 2) % HEAD_DIM == 0
    mask = jnp.where(lane & ~valid[:, :, None], MASKED, 0.0).astype(BF16)
    ones = jnp.where(
        lax.broadcasted_iota(jnp.int32, (2 * SLOTS, PAIR), 1) % HEAD_DIM == 0, 1.0, 0.0
    ).astype(BF16)
    line_of = lambda a: a.reshape(1, -1)

    (queries, keys, values, keep, normed, scaled, inverse), _ = attend(
        pos,
        own_tokens,
        other_tokens,
        mask,
        ones,
        w_qkv,
        line_of(query_bias),
        line_of(value_bias),
        w_out,
        line_of(out_bias),
        line_of(gain_one),
        line_of(shift_one),
    )
    keep_got = core(keep)
    (act_mine, slope, send, out_own, out_other, grad_second, small_two), _ = feed(
        pos,
        normed,
        keep,
        w_up,
        line_of(up_bias),
        w_down,
        line_of(down_bias),
        line_of(gain_two),
        line_of(shift_two),
        own_cot,
        other_cot,
    )
    send_got = core(send)
    out_got = across(out_other)
    back = (send, slope, w_down, w_up)
    (up_theirs, up_bias_theirs, before), done = feed_back(True, pos, *back, (), ())
    up_got = core(up_theirs)

    down_part, done = down_gradient(pos, (act_mine, send_got, send, send_got), (done,))
    down_sum = lax.psum_scatter(
        down_part, "batch", scatter_dimension=0, axis_index_groups=same_core, tiled=True
    )
    (
        (up_mine, up_bias_mine, grad_first, branch_theirs, branch_mine, grad_attended, small_one),
        done,
    ) = feed_back(
        False,
        pos,
        *back,
        (before, grad_second, scaled, inverse, line_of(gain_one), w_out),
        (done,),
    )
    up_ins = (keep, keep_got, up_mine, up_got)
    (up_far, up_across), done = gradient(
        "up", pos, up_ins, ((3, (), (TALL,)), (2, (), (TALL,))), (done, out_got)
    )
    up_far, up_across = across(up_far), across(up_across)
    heads = (pos, mask, ones, queries, keys, values, grad_attended, w_qkv)
    (joint_theirs, before, before_bias), done = attend_back(
        True, *heads, branch_theirs, (grad_first,), (done,)
    )
    joint_got = core(joint_theirs)
    (up_along,), done = gradient(
        "up", pos, up_ins, ((1, ((0, 0),), (TALL,)),), (done,), (up_far,)
    )
    up_along = along(up_along)
    (joint_mine, grad_own, grad_other, small), done = attend_back(
        False,
        *heads,
        branch_mine,
        (before, before_bias, small_one, small_two, up_bias_theirs, up_bias_mine),
        (done,),
    )
    grad_got = across(grad_other)
    mixed_ins = (keep, keep_got, keep, keep_got, joint_mine, joint_got)
    (mixed_low, mixed_high), done = gradient(
        "mixed", pos, mixed_ins, ((3, (), (LOW, LOW)),), (done,)
    )
    mixed_low, mixed_high = along(mixed_low), across(mixed_high)

    by_shares = batch == 16
    shift = lambda a, turn: lax.ppermute(a, "batch", [(i, i ^ (4 * turn)) for i in range(batch)])
    own = ((0, ((0, 0), (1, 0)), SHARES if by_shares else (TALL,)),)

    def swap(shares):
        return [shares[0]] + [shift(shares[turn], turn) for turn in range(1, 4)]

    down_sum, done = sum_of(pos, (down_sum,), (done,))
    down_got = across(down_sum)
    up_sum, done = gradient("up", pos, up_ins, own, (done, grad_got), (up_along, up_across))
    if by_shares:
        up_sum = swap(up_sum)
    else:
        up_sum = lax.psum(up_sum[0], "batch", axis_index_groups=line)
    (mixed_along, mixed_across), done = gradient(
        "mixed",
        pos,
        mixed_ins,
        ((1, ((0, LOW),), (TALL,)), (2, ((1, 0),), (TALL,))),
        (done,),
        (mixed_high, mixed_low),
    )
    mixed_along, mixed_across = along(mixed_along), across(mixed_across)
    down_sum, done = sum_of(pos, (down_sum, down_got), (done,))
    down_half = lax.all_gather(
        down_sum, "batch", axis=0, axis_index_groups=same_core, tiled=True
    )
    if by_shares:
        up_sum, done = sum_of(pos, up_sum, (done,))
        up_sum = swap([up_sum] * 4)
    bit = 1
    while bit < batch:
        small = small + lax.ppermute(small, "batch", [(i, i ^ bit) for i in range(batch)])
        bit *= 2
    small = small + across(small)
    mixed_sum, done = gradient(
        "mixed", pos, mixed_ins, own, (done, small), (mixed_along, mixed_across)
    )
    if by_shares:
        mixed_sum = swap(mixed_sum)
        up_sum, done = join_shares(pos, up_sum, (done,))
    else:
        mixed_sum = lax.psum(mixed_sum[0], "batch", axis_index_groups=line[1:] + line[:1])
    up_x, up_y = along(up_sum), across(up_sum)
    if by_shares:
        mixed_sum, done = sum_of(pos, mixed_sum, (done,))
        mixed_sum = swap([mixed_sum] * 4)
    (layer_output, input_grad), done = place_rows(pos, out_own, out_got, grad_own, grad_got, (done,))
    if by_shares:
        mixed_sum, done = join_shares(pos, mixed_sum, (done,))

    def both(pieces):
        return pieces + [core(p) for p in pieces]

    up_pieces = both([up_sum, up_x, up_y, along(up_y)])
    mixed_x, mixed_y = along(mixed_sum), across(mixed_sum)
    grad_up, done = place(pos, up_pieces, (done,))
    mixed_pieces = both(
        [mixed_sum, mixed_x, mixed_y, across(mixed_x[:LOW]), along(mixed_y[LOW:])]
    )
    grad_down, done = place_down(pos, down_half, core(down_half), (done,))
    (grad_qkv, grad_out), done = place_mixed(pos, mixed_pieces, (done,))
    return (
        layer_output,
        input_grad,
        grad_qkv,
        small[10],
        small[11],
        grad_out,
        small[0],
        grad_up,
        small[6:10].reshape(FF),
        grad_down,
        small[3],
        small[1],
        small[2],
        small[4],
        small[5],
    )


def solution(mesh):
    rows = P("batch", "mod", None)
    return jax.shard_map(
        functools.partial(local, mesh.shape["batch"]),
        mesh=mesh,
        in_specs=(rows, P("batch"), P("batch", None)) + (P(),) * 13 + (rows,),
        out_specs=(rows, rows) + (P(),) * 13,
        check_vma=False,
    )
```

```python
import functools

import jax
import jax.numpy as jnp
from jax import lax
from jax.experimental import pallas as pl
from jax.experimental.pallas import tpu as pltpu
from jax.sharding import PartitionSpec as P

HEADS = 12
HEAD_DIM = 64
WIDTH = 768
FF = 3072
SLOTS = 128
EPSILON = 1e-12
PAIR = 2 * HEAD_DIM
HALF = WIDTH // 2
FF_HALF = FF // 2
CHUNK = 768
CHUNKS = FF // CHUNK
MASKED = -1e30
SCALE = HEAD_DIM ** (-0.5)
MIB = 1 << 20

BF16 = jnp.bfloat16
F32 = jnp.float32


def nn(left, right):
    return lax.dot_general(left, right, (((1,), (0,)), ((), ())), preferred_element_type=F32)


def nt(left, right):
    return lax.dot_general(left, right, (((1,), (1,)), ((), ())), preferred_element_type=F32)


def tn(left, right):
    return lax.dot_general(left, right, (((0,), (0,)), ((), ())), preferred_element_type=F32)


def whole(shape):
    zeros = (0,) * len(shape)
    return pl.BlockSpec(shape, lambda *_: zeros, pipeline_mode=pl.Buffered(1))


TOKEN = (8, 128)
RATE = 10e9


def run(
    body, name, pos, grid, inputs, outputs, us, mib, after=(), scratch=(), aliases={}, carry=()
):
    tokens = len(after)
    riders = len(carry)
    first = 1 + len(inputs)
    outs = first + tokens + riders
    last = outs + len(outputs)
    extra = 2 if carry else 1

    def wrapped(*refs):
        refs[last][...] = jnp.zeros(TOKEN, F32)
        if carry:
            added = [ref[...] for ref in refs[first + tokens : outs]]
            refs[last + 1][...] = sum(added[1:], added[0])
        body(*refs[:first], *refs[outs:last], *refs[last + extra :])

    whole_of = lambda a: whole(a.shape)
    out = pl.pallas_call(
        wrapped,
        grid_spec=pltpu.PrefetchScalarGridSpec(
            num_scalar_prefetch=1,
            grid=grid,
            in_specs=[spec for _, spec in inputs]
            + [pl.BlockSpec(memory_space=pl.ANY)] * tokens
            + [whole_of(a) for a in carry],
            out_specs=[spec for _, _, spec in outputs]
            + [whole(TOKEN)]
            + [whole_of(a) for a in carry[:1]],
            scratch_shapes=list(scratch),
        ),
        out_shape=[jax.ShapeDtypeStruct(shape, kind) for shape, kind, _ in outputs]
        + [jax.ShapeDtypeStruct(TOKEN, F32)]
        + [jax.ShapeDtypeStruct(a.shape, F32) for a in carry[:1]],
        compiler_params=pltpu.CompilerParams(
            dimension_semantics=("arbitrary",) * len(grid), vmem_limit_bytes=mib * MIB
        ),
        cost_estimate=pl.CostEstimate(
            flops=int(us * RATE), bytes_accessed=1000, transcendentals=0
        ),
        input_output_aliases=aliases,
        name=name,
    )(pos, *[array for array, _ in inputs], *after, *carry)
    if carry:
        return out[:-2], out[-2], out[-1]
    return out[:-1], out[-1]


def lane_half(shape):
    return lax.broadcasted_iota(jnp.int32, shape, 1) >= HEAD_DIM


def head_operands(upper, head, query, key, ones, mask):
    if head == 0:
        return jnp.where(upper, ones, query), jnp.where(upper, mask, key)
    return jnp.where(upper, query, ones), jnp.where(upper, key, mask)


def softmax_over_keys(scores):
    exponent = jnp.exp(scores - jnp.max(scores, axis=0, keepdims=True))
    return exponent * (1.0 / jnp.sum(exponent, axis=0, keepdims=True))


def norm(rows):
    center = jnp.mean(rows, axis=-1, keepdims=True)
    centered = rows - center
    variance = jnp.mean(centered * centered, axis=-1, keepdims=True)
    inverse = lax.rsqrt(variance + EPSILON)
    return centered * inverse, inverse


def norm_back(grad_result, scaled, inverse, gain):
    grad_scaled = grad_result * gain
    first_mean = jnp.mean(grad_scaled, axis=-1, keepdims=True)
    second_mean = jnp.mean(grad_scaled * scaled, axis=-1, keepdims=True)
    return inverse * (grad_scaled - first_mean - scaled * second_mean)


GROUP = 384
GROUPS = WIDTH // GROUP
FORWARD = GROUPS
BACKWARD = GROUPS + CHUNKS
STEPS = GROUPS + 2 * CHUNKS
PARTS = 1


def gelu_and_slope(upward):
    size = jnp.abs(upward)
    divisor = 1.0 + (0.3275911 * 0.7071067811865476) * size
    near = pl.reciprocal(divisor, approx=True)
    near = near * (2.0 - divisor * near)
    bell = jnp.exp(-0.5 * upward * upward)
    poly = 0.5 * 1.061405429 * near - 0.5 * 1.453152027
    poly = poly * near + 0.5 * 1.421413741
    poly = poly * near - 0.5 * 0.284496736
    poly = poly * near + 0.5 * 0.254829592
    tail = poly * near * bell
    phi = jnp.where(upward >= 0, 1.0 - tail, tail)
    return upward * phi, phi + upward * (bell * 0.3989422804014327)


def layer_body(
    items,
    pos,
    own,
    other,
    mask,
    ones,
    w_q,
    w_k,
    w_v,
    query_bias,
    value_bias,
    w_out,
    out_bias,
    gain_one,
    shift_one,
    w_up,
    up_bias,
    w_down,
    down_bias,
    gain_two,
    shift_two,
    cot_own,
    cot_other,
    queries,
    keys,
    values,
    keep,
    act_mine,
    send,
    out_own,
    out_other,
    up_theirs,
    up_mine,
    up_bias_grad,
    grad_first,
    branch_theirs,
    branch_mine,
    grad_attended,
    small,
    total,
    attended,
    slope,
    normed,
    scaled,
    inverse,
    grad_second,
    branch,
):
    step = pl.program_id(0)
    span = 2 * SLOTS
    count = items * span
    rows_out = keep.at[0]
    part = count // PARTS
    parts = [slice(i * part, (i + 1) * part) for i in range(PARTS)]

    @pl.when(step == 0)
    def _():
        for item in range(items):
            rows_out[item * span : item * span + SLOTS, :] = own[item]
            rows_out[item * span + SLOTS : (item + 1) * span, :] = other[item]
        total[...] = jnp.zeros_like(total)

    @pl.when(step < FORWARD)
    def _():
        rows = rows_out[...]
        queries[...] = (nn(rows, w_q[...]) + query_bias[...]).astype(BF16)
        keys[...] = nn(rows, w_k[...]).astype(BF16)
        values[...] = (nn(rows, w_v[...]) + value_bias[...]).astype(BF16)
        upper = lane_half((span, PAIR))
        for item in range(items):
            at = slice(item * span, (item + 1) * span)
            for pair in range(GROUP // PAIR):
                cols = slice(pair * PAIR, (pair + 1) * PAIR)
                query = queries[at, cols] * jnp.asarray(SCALE, BF16)
                key = keys[at, cols]
                value = values[at, cols]
                heads = []
                for head in range(2):
                    query_h, key_h = head_operands(
                        upper, head, query, key, ones[...], mask[item]
                    )
                    probs = softmax_over_keys(nt(key_h, query_h))
                    heads.append(tn(probs.astype(BF16), value))
                attended[at, cols] = jnp.where(upper, heads[1], heads[0]).astype(BF16)
        place = pl.ds(pl.multiple_of(step * GROUP, GROUP), GROUP)
        total[...] += nn(attended[...], w_out[place, :])
        keep[1, :, place] = attended[...]

    @pl.when(step == FORWARD - 1)
    def _():
        summed = rows_out[...].astype(F32) + (total[...] + out_bias[...])
        unit, inv = norm(summed)
        result = unit * gain_one[...] + shift_one[...]
        scaled[...] = unit
        inverse[...] = inv
        normed[...] = result
        keep[2] = result.astype(BF16)
        total[...] = jnp.zeros_like(total)

    @pl.when((step >= FORWARD) & (step < BACKWARD))
    def _():
        chunk = step - FORWARD
        cols = pl.ds(pl.multiple_of(lax.rem(chunk, CHUNKS // 2) * CHUNK, CHUNK), CHUNK)
        ups = [nn(keep[2, at, :], w_up[...]) + up_bias[...] for at in parts]
        for at, upward in zip(parts, ups):
            active, steep = gelu_and_slope(upward)
            slope[chunk, at, :] = steep
            active = active.astype(BF16)

            @pl.when(chunk < CHUNKS // 2)
            def _(active=active, at=at):
                send[at, cols] = active

            @pl.when(chunk >= CHUNKS // 2)
            def _(active=active, at=at):
                act_mine[at, :] = active

            total[at, :] += nn(active, w_down[...])

    @pl.when(step == BACKWARD - 1)
    def _():
        unit, inv = norm(normed[...] + (total[...] + down_bias[...]))
        result = (unit * gain_two[...] + shift_two[...]).astype(BF16)
        cots = []
        for item in range(items):
            out_own[item] = result[item * span : item * span + SLOTS]
            out_other[item] = result[item * span + SLOTS : (item + 1) * span]
            cots += [cot_own[item], cot_other[item]]
        cot = jnp.concatenate(cots, axis=0).astype(F32)
        grad = norm_back(cot, unit, inv, gain_two[...])
        low = grad.astype(BF16)
        grad_second[...] = grad
        send[:, FF_HALF:] = low
        small[...] = jnp.zeros_like(small)
        small[3:4, :] = jnp.sum(low.astype(F32), axis=0, keepdims=True)
        small[4:5, :] = jnp.sum(cot * unit, axis=0, keepdims=True)
        small[5:6, :] = jnp.sum(cot, axis=0, keepdims=True)
        total[...] = grad

    @pl.when(step >= BACKWARD)
    def _():
        chunk = step - BACKWARD
        place = pl.multiple_of(half_chunk(chunk, pos) * CHUNK, CHUNK)
        downs = [nt(send[at, FF_HALF:], w_down[...]) for at in parts]
        sums = []
        for at, down in zip(parts, downs):
            low = (down * slope[chunk, at, :]).astype(BF16)

            @pl.when(chunk < CHUNKS // 2)
            def _(low=low, at=at):
                up_theirs[at, :] = low

            @pl.when(chunk >= CHUNKS // 2)
            def _(low=low, at=at):
                up_mine[at, :] = low

            sums.append(jnp.sum(low.astype(F32), axis=0, keepdims=True))
            total[at, :] += nt(low, w_up[...])
        up_bias_grad[:, pl.ds(place, CHUNK)] = sum(sums[1:], sums[0])

    @pl.when(step == STEPS - 1)
    def _():
        grad_normed = total[...]
        unit = scaled[...]
        grad = norm_back(grad_normed, unit, inverse[...], gain_one[...])
        grad_first[...] = grad
        branch[...] = grad.astype(BF16)
        mine = pl.multiple_of(pos[0] * HALF, HALF)
        theirs = pl.multiple_of((1 - pos[0]) * HALF, HALF)
        branch_mine[...] = branch[:, pl.ds(mine, HALF)]
        branch_theirs[...] = branch[:, pl.ds(theirs, HALF)]
        grad_attended[...] = nt(branch[...], w_out[...]).astype(BF16)
        small[0:1, :] = jnp.sum(branch[...].astype(F32), axis=0, keepdims=True)
        small[1:2, :] = jnp.sum(grad_normed * unit, axis=0, keepdims=True)
        small[2:3, :] = jnp.sum(grad_normed, axis=0, keepdims=True)


def half_chunk(j, pos):
    return lax.rem(j + (1 - pos[0]) * (CHUNKS // 2), CHUNKS)


def layer(
    pos,
    own,
    other,
    mask,
    ones,
    w_qkv,
    query_bias,
    value_bias,
    w_out,
    out_bias,
    gain_one,
    shift_one,
    w_up,
    up_bias,
    w_down,
    down_bias,
    gain_two,
    shift_two,
    cot_own,
    cot_other,
):
    items = own.shape[0]
    count = items * 2 * SLOTS
    half = CHUNKS // 2
    group = lambda j: jnp.minimum(j, GROUPS - 1)
    between = lambda j, first: jnp.clip(j - first, 0, half - 1)

    def chunk(j, pos):
        return half_chunk(
            jnp.where(j < BACKWARD, jnp.maximum(j - FORWARD, 0), j - BACKWARD), pos
        )

    row = pl.BlockSpec((1, GROUP), lambda j, pos: (0, group(j)))
    flat = pl.BlockSpec((count, GROUP), lambda j, pos: (0, group(j)))
    hidden = lambda first: pl.BlockSpec((count, CHUNK), lambda j, pos: (0, between(j, first)))
    weight = lambda k: pl.BlockSpec((WIDTH, GROUP), lambda j, pos: (0, k * GROUPS + group(j)))
    vector = whole((1, WIDTH))
    rows = whole(own.shape)
    shape = (count, WIDTH)
    full = whole(shape)
    narrow = whole((count, HALF))
    return run(
        functools.partial(layer_body, items),
        "layer",
        pos,
        (STEPS,),
        [
            (own, rows),
            (other, rows),
            (mask, whole(mask.shape)),
            (ones, whole(ones.shape)),
            (w_qkv, weight(0)),
            (w_qkv, weight(1)),
            (w_qkv, weight(2)),
            (query_bias, row),
            (value_bias, row),
            (w_out, whole((WIDTH, WIDTH))),
            (out_bias, vector),
            (gain_one, vector),
            (shift_one, vector),
            (w_up, pl.BlockSpec((WIDTH, CHUNK), lambda j, pos: (0, chunk(j, pos)))),
            (up_bias, pl.BlockSpec((1, CHUNK), lambda j, pos: (0, chunk(j, pos)))),
            (w_down, pl.BlockSpec((CHUNK, WIDTH), lambda j, pos: (chunk(j, pos), 0))),
            (down_bias, vector),
            (gain_two, vector),
            (shift_two, vector),
            (cot_own, rows),
            (cot_other, rows),
        ],
        [
            (shape, BF16, flat),
            (shape, BF16, flat),
            (shape, BF16, flat),
            ((3,) + shape, BF16, whole((3,) + shape)),
            ((count, FF_HALF), BF16, hidden(FORWARD + half)),
            ((count, FF_HALF + WIDTH), BF16, whole((count, FF_HALF + WIDTH))),
            (own.shape, BF16, rows),
            (own.shape, BF16, rows),
            ((count, FF_HALF), BF16, hidden(BACKWARD)),
            ((count, FF_HALF), BF16, hidden(BACKWARD + half)),
            ((1, FF), F32, whole((1, FF))),
            (shape, F32, full),
            ((count, HALF), BF16, narrow),
            ((count, HALF), BF16, narrow),
            (shape, BF16, full),
            ((8, WIDTH), F32, whole((8, WIDTH))),
        ],
        scratch=[
            pltpu.VMEM(shape, F32),
            pltpu.VMEM((count, GROUP), BF16),
            pltpu.VMEM((CHUNKS, count, CHUNK), F32),
            pltpu.VMEM(shape, F32),
            pltpu.VMEM(shape, F32),
            pltpu.VMEM((count, 1), F32),
            pltpu.VMEM(shape, F32),
            pltpu.VMEM(shape, BF16),
        ],
        us=30,
        mib=56,
    )


def keep_rows(which, count, cols, place):
    return pl.BlockSpec((None, count, cols), lambda j, pos: (which, 0, place(j, pos)))


def attend_back_half(
    items, mask, ones, queries, keys, values, grad_attended, w_q, w_k, w_v, joined
):
    span = 2 * SLOTS
    upper = lane_half((span, PAIR))
    for item in range(items):
        at = slice(item * span, (item + 1) * span)
        for pair in range(HALF // PAIR):
            cols = slice(pair * PAIR, (pair + 1) * PAIR)
            query = queries[at, cols] * jnp.asarray(SCALE, BF16)
            key = keys[at, cols]
            value = values[at, cols]
            grad_out = grad_attended[at, cols]
            none = jnp.zeros_like(grad_out)
            grads = []
            for head in range(2):
                query_h, key_h = head_operands(
                    upper, head, query, key, ones[...], mask[item]
                )
                probs = softmax_over_keys(nt(key_h, query_h))
                if head == 0:
                    grad_h = jnp.where(upper, none, grad_out)
                else:
                    grad_h = jnp.where(upper, grad_out, none)
                grad_probs = nt(value, grad_h)
                inner = jnp.sum(probs * grad_probs, axis=0, keepdims=True)
                grad_scores = (probs * (grad_probs - inner)).astype(BF16)
                grads.append(
                    (
                        tn(grad_scores, key) * SCALE,
                        nn(grad_scores, query),
                        nn(probs.astype(BF16), grad_out),
                    )
                )
            for index in range(3):
                place = slice(index * HALF + pair * PAIR, index * HALF + (pair + 1) * PAIR)
                joined[at, place] = jnp.where(
                    upper, grads[1][index], grads[0][index]
                ).astype(BF16)
    parts = [joined[:, index * HALF : (index + 1) * HALF] for index in range(3)]
    sums = [jnp.sum(parts[index].astype(F32), axis=0, keepdims=True) for index in (0, 2)]
    total = nt(parts[0], w_q[...]) + nt(parts[1], w_k[...]) + nt(parts[2], w_v[...])
    return total, sums


def attend_back_body(items, pos, *refs):
    *ins, first, second, grad_first, small_in, up_bias, theirs, mine, own, other, small, total, joined = refs
    step = pl.program_id(0)
    span = 2 * SLOTS
    part, sums = attend_back_half(items, *ins, joined)

    @pl.when(step == 0)
    def _():
        theirs[:, : 3 * HALF] = joined[...]
        theirs[:, 3 * HALF :] = first[...]
        total[...] = grad_first[...] + part
        small[...] = jnp.zeros_like(small)
        small[0:8, :] = small_in[...]
        for index in range(FF // WIDTH):
            small[6 + index : 7 + index, :] = up_bias[:, index * WIDTH : (index + 1) * WIDTH]

    @pl.when(step == 1)
    def _():
        mine[:, : 3 * HALF] = joined[...]
        mine[:, 3 * HALF :] = second[...]
        for item in range(items):
            at = slice(item * span, item * span + SLOTS)
            own[item] = total[at, :] + part[at]
            at = slice(item * span + SLOTS, (item + 1) * span)
            other[item] = (total[at, :] + part[at]).astype(BF16)

    place = pl.multiple_of(lax.rem(step + 1 + pos[0], 2) * HALF, HALF)
    for index in range(2):
        small[10 + index : 11 + index, pl.ds(place, HALF)] = sums[index]


def attend_back(
    pos, mask, ones, queries, keys, values, grad_attended, w_qkv, first, second, grad_first, small, up_bias, after
):
    count = queries.shape[0]
    items = mask.shape[0]
    half = lambda j, pos: lax.rem(j + 1 + pos[0], 2)
    flat = pl.BlockSpec((count, HALF), lambda j, pos: (0, half(j, pos)))
    weight = lambda k: pl.BlockSpec((WIDTH, HALF), lambda j, pos: (0, 2 * k + half(j, pos)))
    joined = ((count, 4 * HALF), BF16, whole((count, 4 * HALF)))
    rows = whole((items, SLOTS, WIDTH))
    return run(
        functools.partial(attend_back_body, items),
        "attend_back",
        pos,
        (2,),
        [
            (mask, whole(mask.shape)),
            (ones, whole(ones.shape)),
            (queries, flat),
            (keys, flat),
            (values, flat),
            (grad_attended, flat),
            (w_qkv, weight(0)),
            (w_qkv, weight(1)),
            (w_qkv, weight(2)),
        ]
        + [(a, whole(a.shape)) for a in (first, second, grad_first, small, up_bias)],
        [
            joined,
            joined,
            ((items, SLOTS, WIDTH), F32, rows),
            ((items, SLOTS, WIDTH), BF16, rows),
            ((16, WIDTH), F32, whole((16, WIDTH))),
        ],
        after=after,
        scratch=[pltpu.VMEM((count, WIDTH), F32), pltpu.VMEM((count, 3 * HALF), BF16)],
        us=12,
        mib=32,
    )


TALL = HALF
LOW = TALL // 2
FAR, ACROSS, ALONG, OWN = 3, 2, 1, 0
PIECE = (TALL, WIDTH)


def quarter(pos, there):
    return pos[1] ^ (there >> 1), pos[2] ^ (there & 1)


def order_of(kind, step):
    first, second = (ACROSS, ALONG) if kind == "up" else (ALONG, ACROSS)
    return jnp.where(step == 0, FAR, jnp.where(step == 1, first, jnp.where(step == 2, second, OWN)))


def gradient_body(kind, block, outs, pos, *refs):
    ins, outs = refs[:-outs], refs[-outs:]
    step = pl.program_id(0)
    value = block(quarter(pos, order_of(kind, step))[1], *ins).astype(BF16)
    if kind == "mixed":
        targets = [None, outs[2], outs[3], outs[4]]
    else:
        targets = [outs[0].at[0], outs[0].at[1], outs[1], outs[2]]
    for index, target in enumerate(targets):

        @pl.when(step == index)
        def _(target=target):
            if target is None:
                outs[0][...] = value[:LOW]
                outs[1][...] = value[LOW:]
            else:
                target[...] = value


def plain_block(along, left_a, left_b, right_a, right_b):
    return tn(left_a[...], right_a[...]) + tn(left_b[...], right_b[...])


def mixed_block(along, rows_a, rows_b, att_a, att_b, right_a, right_b):
    left_a = jnp.where(along == 0, rows_a[...], att_a[...])
    left_b = jnp.where(along == 0, rows_b[...], att_b[...])
    return jnp.concatenate(
        [
            tn(rows_a[...], right_a[:, :HALF]) + tn(rows_b[...], right_b[:, :HALF]),
            tn(left_a, right_a[:, HALF:]) + tn(left_b, right_b[:, HALF:]),
        ],
        axis=1,
    )


def gradient(kind, pos, operands, after):
    count = operands[-1].shape[0]
    across = lambda j, pos: quarter(pos, order_of(kind, j))[0]
    along = lambda j, pos: quarter(pos, order_of(kind, j))[1]
    block = plain_block
    if kind == "down":
        lefts = pl.BlockSpec(
            (count, TALL), lambda j, pos: (0, 2 * across(j, pos) + along(j, pos))
        )
        rights = pl.BlockSpec((count, WIDTH), lambda j, pos: (0, FF_HALF // WIDTH))
        specs = [lefts, lefts, rights, rights]
    else:
        rights = pl.BlockSpec((count, WIDTH), lambda j, pos: (0, along(j, pos)))
        if kind == "up":
            lefts = keep_rows(2, count, TALL, across)
            specs = [lefts, lefts, rights, rights]
        else:
            rows, att = keep_rows(0, count, TALL, across), keep_rows(1, count, TALL, across)
            specs = [rows, rows, att, att, rights, rights]
            block = mixed_block
    if kind == "mixed":
        shapes = [(LOW, WIDTH)] * 2 + [PIECE] * 3
    else:
        shapes = [(2,) + PIECE] + [PIECE] * 2
    return run(
        functools.partial(gradient_body, kind, block, len(shapes)),
        kind + "_gradient",
        pos,
        (4,),
        list(zip(operands, specs)),
        [(shape, BF16, whole(shape)) for shape in shapes],
        after=after,
        us=5,
        mib=20,
    )


def sum_body(share, pos, *refs):
    ins = refs[:-3] if share else refs[:-1]
    total = ins[0][...].astype(F32)
    for ref in ins[1:]:
        total = total + ref[...].astype(F32)
    if not share:
        refs[-1][...] = total.astype(BF16)
        return
    held = refs[-1]
    held[...] = total
    for turn in range(2):
        first = pl.multiple_of((pos[3] ^ turn) * LOW, LOW)
        refs[turn - 3][...] = held[pl.ds(first, LOW), :].astype(BF16)


def sum_of(pos, arrays, after, share=False, carry=(), us=1):
    shape = arrays[0].shape
    item = lambda index: pl.BlockSpec((None,) + PIECE, lambda *_: (index, 0, 0))
    shapes = [(LOW, WIDTH)] * 2 if share else [shape]
    out, *more = run(
        functools.partial(sum_body, share),
        "sum_shares" if share else "sum_of",
        pos,
        (1,),
        [
            (a[0], item(a[1])) if isinstance(a, tuple) else (a, whole(shape))
            for a in arrays
        ],
        [(shape, BF16, whole(shape)) for shape in shapes],
        after=after,
        scratch=[pltpu.VMEM(shape, F32)] if share else [],
        us=us,
        mib=8,
        carry=carry,
    )
    return (out if share else out[0]), *more


def sides_body(pos, along, across, low, high, along_out, across_out):
    along_out[:LOW, :] = along[:LOW, :]
    along_out[LOW:, :] = (along[LOW:, :].astype(F32) + high[...].astype(F32)).astype(BF16)
    across_out[:LOW, :] = (across[:LOW, :].astype(F32) + low[...].astype(F32)).astype(BF16)
    across_out[LOW:, :] = across[LOW:, :]


def sum_sides(pos, along, across, low, high, after, carry=()):
    return run(
        sides_body,
        "sum_sides",
        pos,
        (1,),
        [(a, whole(a.shape)) for a in (along, across, low, high)],
        [(PIECE, BF16, whole(PIECE))] * 2,
        after=after,
        carry=carry,
        us=0.1,
        mib=8,
    )


def split_body(pos, own, first, second, low, high, packed):
    low[...] = first[:LOW, :]
    high[...] = second[LOW:, :]
    for index, ref in enumerate((own, first, second)):
        packed[index] = ref[...]


def split(pos, own, first, second, after):
    half = (LOW, WIDTH)
    return run(
        split_body,
        "split",
        pos,
        (1,),
        [(a, whole(PIECE)) for a in (own, first, second)],
        [(half, BF16, whole(half))] * 2 + [((3,) + PIECE, BF16, whole((3,) + PIECE))],
        after=after,
        us=1,
        mib=10,
    )


def pack_body(pos, *refs):
    for index, ref in enumerate(refs[:-1]):
        refs[-1][index] = ref[...]


def pack(pos, pieces, after):
    shape = (len(pieces),) + PIECE
    out, token = run(
        pack_body,
        "pack",
        pos,
        (1,),
        [(a, whole(PIECE)) for a in pieces],
        [(shape, BF16, whole(shape))],
        after=after,
        us=0.1,
        mib=12,
    )
    return out[0], token


def stack_halves(pos, low, high, after):
    half = (LOW, WIDTH)
    out, token = run(
        pack_body,
        "stack_halves",
        pos,
        (1,),
        [(low, whole(half)), (high, whole(half))],
        [((2,) + half, BF16, whole((2,) + half))],
        after=after,
        us=0.1,
        mib=6,
    )
    return out[0], token


def join_body(pos, mine, theirs, out):
    for turn, ref in enumerate((mine, theirs)):
        first = pl.multiple_of((pos[3] ^ turn) * LOW, LOW)
        out[pl.ds(first, LOW), :] = ref[...]


def join_shares(pos, shares, after, carry=()):
    out, *more = run(
        join_body,
        "join_shares",
        pos,
        (1,),
        [(a, whole(a.shape)) for a in shares],
        [(PIECE, BF16, whole(PIECE))],
        after=after,
        us=0.1,
        mib=6,
        carry=carry,
    )
    return out[0], *more


def place_body(kind, entries, outs, pos, *refs):
    sources = iter(refs)
    pieces = []
    for _, _, _, _, index in entries:
        if not index:
            ref = next(sources)
        pieces.append(ref if index is None else ref.at[index])
    targets = refs[len(refs) - 4 - outs : len(refs) - 4]
    taken, given, in_sems, out_sems = refs[-4:]
    fetches = []
    for index, (rows, *_) in enumerate(entries):
        fetch = pltpu.make_async_copy(
            pieces[index], taken.at[index, pl.ds(0, rows)], in_sems.at[index]
        )
        fetch.start()
        fetches.append(fetch)

    def sends(index):
        rows, theirs, there, start, _ = entries[index]
        half = pos[0] ^ theirs
        across, along = quarter(pos, there)
        source = given.at[index]
        if kind == "down":
            first = pl.multiple_of((4 * half + 2 * across + along) * TALL + start, LOW)
            yield None, source.at[pl.ds(0, rows)], targets[0].at[pl.ds(first, rows)], 0
            return
        first = pl.multiple_of(across * TALL + start, LOW)
        if kind == "up":
            column = pl.multiple_of((2 * half + along) * WIDTH, WIDTH)
            target = targets[0].at[pl.ds(first, rows), pl.ds(column, WIDTH)]
            yield None, source.at[pl.ds(0, rows)], target, 0
            return
        for part in range(2):
            source_part = source.at[pl.ds(0, rows), pl.ds(part * HALF, HALF)]
            column = pl.multiple_of(jnp.minimum(2 * along + part, 2) * WIDTH + half * HALF, HALF)
            target = targets[0].at[pl.ds(first, rows), pl.ds(column, HALF)]
            if part == 0:
                yield None, source_part, target, 0
            else:
                yield along == 0, source_part, target, 1
                column = pl.multiple_of(half * HALF, HALF)
                target = targets[1].at[pl.ds(first, rows), pl.ds(column, HALF)]
                yield along == 1, source_part, target, 1

    def each(index, act):
        for condition, source, target, sem in sends(index):
            copy = pltpu.make_async_copy(source, target, out_sems.at[index, sem])
            if condition is None:
                act(copy)
            else:

                @pl.when(condition)
                def _(copy=copy):
                    act(copy)

    for index, (rows, *_) in enumerate(entries):
        fetches[index].wait()
        given[index, :rows, :] = taken[index, :rows, :].astype(F32)
        each(index, lambda copy: copy.start())
    for index in range(len(entries)):
        each(index, lambda copy: copy.wait())


def place(kind, pos, pieces, before, after):
    pieces = [piece if len(piece) == 5 else piece + (None,) for piece in pieces]
    entries = tuple((p.shape[-2],) + tuple(more) for p, *more in pieces)
    shapes = {
        "down": [(FF, WIDTH)],
        "up": [(WIDTH, FF)],
        "mixed": [(WIDTH, 3 * WIDTH), (WIDTH, WIDTH)],
    }[kind]
    anywhere = pl.BlockSpec(memory_space=pl.ANY)
    arrays = [p for p, *_, index in pieces if not index]
    ins = [(a, anywhere) for a in arrays + list(before)]
    count = len(entries)
    return run(
        functools.partial(place_body, kind, entries, len(shapes)),
        "place_" + kind,
        pos,
        (1,),
        ins,
        [(shape, F32, anywhere) for shape in shapes],
        after=after,
        scratch=[
            pltpu.VMEM((count, TALL, WIDTH), BF16),
            pltpu.VMEM((count, TALL, WIDTH), F32),
            pltpu.SemaphoreType.DMA((count,)),
            pltpu.SemaphoreType.DMA((count, 2)),
        ],
        aliases={1 + len(arrays) + index: index for index in range(len(before))},
        us=0.02,
        mib=22,
    )


def place_rows_body(pos, own, got, own_grad, got_grad, out, grad):
    @pl.when(pl.program_id(0) == 0)
    def _():
        out[...] = own[...]
        grad[...] = own_grad[...]

    @pl.when(pl.program_id(0) == 1)
    def _():
        out[...] = got[...]
        grad[...] = got_grad[...].astype(F32)


def place_rows(pos, own, got, own_grad, got_grad, after):
    items = own.shape[0]
    spec = pl.BlockSpec(own.shape, lambda step, pos: (pos[1] ^ step, 0, 0))
    shape = (2 * items,) + own.shape[1:]
    return run(
        place_rows_body,
        "place_rows",
        pos,
        (2,),
        [(a, whole(own.shape)) for a in (own, got, own_grad, got_grad)],
        [(shape, BF16, spec), (shape, F32, spec)],
        after=after,
        us=0.02,
        mib=10,
    )


def local(
    batch,
    tokens,
    caption_lengths,
    region_mask,
    w_qkv,
    query_bias,
    value_bias,
    w_out,
    out_bias,
    w_up,
    up_bias,
    w_down,
    down_bias,
    gain_one,
    shift_one,
    gain_two,
    shift_two,
    cotangent,
):
    swap_core = [(i, i ^ 1) for i in range(batch)]
    swap_along = [(i, i ^ 2) for i in range(batch)]
    swap_across = [(0, 1), (1, 0)]
    line = [[4 * k + i for k in range(batch // 4)] for i in range(4)]
    same_core = [[2 * k + i for k in range(batch // 2)] for i in range(2)]
    core = lambda a: lax.ppermute(a, "batch", swap_core)
    along = lambda a: lax.ppermute(a, "batch", swap_along)
    across = lambda a: lax.ppermute(a, "mod", swap_across)

    place_y = lax.axis_index("mod")
    place_b = lax.axis_index("batch")
    pos = jnp.stack([place_b % 2, place_y, (place_b // 2) % 2, (place_b // 4) % 2]).astype(jnp.int32)
    items = tokens.shape[0] // 2
    mine = place_y * items
    rest = (1 - place_y) * items
    rows = lambda a, start: lax.dynamic_slice_in_dim(a, start, items, axis=0)

    other_tokens = across(rows(tokens, rest))
    other_cot = across(rows(cotangent, rest))
    own_tokens = rows(tokens, mine)
    own_cot = rows(cotangent, mine)

    slot = lax.broadcasted_iota(jnp.int32, (items, SLOTS), 1)
    text = slot < rows(caption_lengths, mine)[:, None]
    region = rows(region_mask, mine) > 0
    valid = jnp.concatenate(
        [jnp.where(place_y == 0, text, region), jnp.where(place_y == 0, region, text)], axis=1
    )
    lane = lax.broadcasted_iota(jnp.int32, (1, 1, PAIR), 2) % HEAD_DIM == 0
    mask = jnp.where(lane & ~valid[:, :, None], MASKED, 0.0).astype(BF16)
    ones = jnp.where(
        lax.broadcasted_iota(jnp.int32, (2 * SLOTS, PAIR), 1) % HEAD_DIM == 0, 1.0, 0.0
    ).astype(BF16)
    line_of = lambda a: a.reshape(1, -1)

    (
        (
            queries,
            keys,
            values,
            keep,
            act_mine,
            send,
            out_own,
            out_other,
            up_theirs,
            up_mine,
            up_bias_grad,
            grad_first,
            branch_theirs,
            branch_mine,
            grad_attended,
            small,
        ),
        done,
    ) = layer(
        pos,
        own_tokens,
        other_tokens,
        mask,
        ones,
        w_qkv,
        line_of(query_bias),
        line_of(value_bias),
        w_out,
        line_of(out_bias),
        line_of(gain_one),
        line_of(shift_one),
        w_up,
        line_of(up_bias),
        w_down,
        line_of(down_bias),
        line_of(gain_two),
        line_of(shift_two),
        own_cot,
        other_cot,
    )
    send_got, keep_got, up_got = core(send), core(keep), core(up_theirs)
    out_got = across(out_other)
    by_shares = batch == 16
    near = lambda a: lax.ppermute(a, "batch", [(i, i ^ 4) for i in range(batch)])
    wide = lambda a: lax.ppermute(a, "batch", [(i, i ^ 8) for i in range(batch)])

    def line_sum(piece, turn):
        return lax.psum(piece, "batch", axis_index_groups=line[turn:] + line[:turn])

    hops = [across]
    bit = 2
    while bit < batch:
        hops.append(
            lambda a, bit=bit: lax.ppermute(a, "batch", [(i, i ^ bit) for i in range(batch)])
        )
        bit *= 2
    hops.append(core)

    def ride(kernel, *args, **more):
        nonlocal small, got, riding
        if not riding:
            return kernel(*args, **more)
        out, done, small = kernel(
            *args, **more, carry=(small,) if got is None else (small, got)
        )
        got = hops.pop(0)(small) if hops else None
        return out, done

    (down_pair, down_across, down_own), done = gradient(
        "down", pos, (act_mine, send_got, send, send_got), (done,)
    )
    down_pair = along(down_pair)
    (up_pair, up_along, up_own), done = gradient(
        "up", pos, (keep, keep_got, up_mine, up_got), (done, out_got)
    )
    up_pair = across(up_pair)
    (joint_theirs, joint_mine, grad_own, grad_other, small), done = attend_back(
        pos,
        mask,
        ones,
        queries,
        keys,
        values,
        grad_attended,
        w_qkv,
        branch_theirs,
        branch_mine,
        grad_first,
        small,
        up_bias_grad,
        (done,),
    )
    joint_got = core(joint_theirs)
    down_across, done = sum_of(pos, (down_across, (down_pair, 0)), (done,))
    down_across = across(down_across)
    up_along, done = sum_of(pos, (up_along, (up_pair, 0)), (done,))
    up_along = along(up_along)
    (mixed_low, mixed_high, mixed_along, mixed_across, mixed_own), done = gradient(
        "mixed", pos, (keep, keep_got, keep, keep_got, joint_mine, joint_got), (done,)
    )
    mixed_low, mixed_high = along(mixed_low), across(mixed_high)
    got, riding = None, False

    def halves(arrays, done, turn):
        parts, done = ride(sum_of, pos, arrays, (done,), share=by_shares, us=0.1)
        if by_shares:
            return (parts[0], near(parts[1])), done
        return line_sum(parts, turn), done

    def widen(parts, after):
        if not by_shares:
            return parts, after[0]
        half, done = ride(sum_of, pos, parts, after, us=0.1)
        return (half, wide(half)), done

    def narrow(parts, after):
        if not by_shares:
            return parts, after[0]
        half, done = ride(sum_of, pos, parts, after, us=0.1)
        return (half, near(half)), done

    def joined(parts, after):
        return ride(join_shares, pos, parts, after) if by_shares else (parts, after[0])

    down_sum, done = halves((down_own, (down_pair, 1), down_across), done, 0)
    up_sum, done = halves((up_own, (up_pair, 1), up_along), done, 1)
    (mixed_along, mixed_across), done = ride(
        sum_sides, pos, mixed_along, mixed_across, mixed_low, mixed_high, (done,)
    )
    mixed_along, mixed_across = along(mixed_along), across(mixed_across)
    down_sum, done = widen(down_sum, (done,))
    riding = True
    down_sum, done = narrow(down_sum, (done,))
    up_sum, done = widen(up_sum, (done,))
    mixed_sum, done = halves((mixed_own, mixed_along, mixed_across), done, 2)
    grad_got = across(grad_other)
    down_sum, done = joined(down_sum, (done, grad_got))
    down_x, down_y = along(down_sum), across(down_sum)
    up_sum, done = narrow(up_sum, (done,))
    mixed_sum, done = widen(mixed_sum, (done, down_x, down_y))
    up_sum, done = joined(up_sum, (done,))
    up_x, up_y = along(up_sum), across(up_sum)
    mixed_sum, done = narrow(mixed_sum, (done, up_x, up_y))
    while hops or got is not None:
        small = small + (hops.pop(0)(small) if got is None else got)
        got = None
    vectors = [small[index] for index in range(12)]
    vectors[6] = small[6:10].reshape(FF)
    seen = tuple(vectors[index] for index in (0, 1, 2, 3, 4, 5, 6, 10, 11))
    down_pack, done = pack(pos, (down_sum, down_x, down_y, across(down_x)), (done,))
    mixed_sum, done = joined(mixed_sum, (done,))
    mixed_x, mixed_y = along(mixed_sum), across(mixed_sum)
    up_pack, done = pack(pos, (up_sum, up_x, up_y, along(up_y)), (done,))
    (layer_output, input_grad), done = place_rows(
        pos, out_own, out_got, grad_own, grad_got, (done,)
    )
    def both(pieces):
        return [(p, 0, there, start) for p, there, start in pieces] + [
            (core(p), 1, there, start) for p, there, start in pieces
        ]

    def packed(pieces):
        places = list(enumerate((OWN, ALONG, ACROSS, FAR)))[: pieces.shape[0]]
        return [
            (array, theirs, there, 0, index)
            for theirs, array in enumerate((pieces, core(pieces)))
            for index, there in places
        ]

    (grad_down,), done = place(
        "down",
        pos,
        packed(down_pack),
        (),
        (done,),
    )
    (grad_up,), done = place(
        "up",
        pos,
        packed(up_pack),
        (),
        (done,),
    )
    (mixed_low, mixed_high, mixed_pack), done = split(pos, mixed_sum, mixed_x, mixed_y, (done,))
    mixed_low, mixed_high = across(mixed_low), along(mixed_high)
    partial, done = place(
        "mixed",
        pos,
        packed(mixed_pack),
        (),
        (done,),
    )
    last, done = stack_halves(pos, mixed_low, mixed_high, (done,) + seen)
    ends = [
        (array, theirs, FAR, start, index)
        for theirs, array in enumerate((last, core(last)))
        for index, start in enumerate((0, LOW))
    ]
    (grad_qkv, grad_out), done = place("mixed", pos, ends, partial, (done,))
    return (
        layer_output,
        input_grad,
        grad_qkv,
        vectors[10],
        vectors[11],
        grad_out,
        vectors[0],
        grad_up,
        vectors[6],
        grad_down,
        vectors[3],
        vectors[1],
        vectors[2],
        vectors[4],
        vectors[5],
    )


def solution(mesh):
    rows = P("batch", "mod", None)
    return jax.shard_map(
        functools.partial(local, mesh.shape["batch"]),
        mesh=mesh,
        in_specs=(rows, P("batch"), P("batch", None)) + (P(),) * 13 + (rows,),
        out_specs=(rows, rows) + (P(),) * 13,
        check_vma=False,
    )
```

```python
import functools

import jax
import jax.numpy as jnp
from jax import lax
from jax.experimental import pallas as pl
from jax.experimental.pallas import tpu as pltpu
from jax.sharding import PartitionSpec as P

HEADS = 12
HEAD_DIM = 64
WIDTH = 768
FF = 3072
SLOTS = 128
EPSILON = 1e-12
PAIR = 2 * HEAD_DIM
HALF = WIDTH // 2
FF_HALF = FF // 2
CHUNK = 768
CHUNKS = FF // CHUNK
MASKED = -1e30
SCALE = HEAD_DIM ** (-0.5)
MIB = 1 << 20

BF16 = jnp.bfloat16
F32 = jnp.float32


def nn(left, right):
    return lax.dot_general(left, right, (((1,), (0,)), ((), ())), preferred_element_type=F32)


def nt(left, right):
    return lax.dot_general(left, right, (((1,), (1,)), ((), ())), preferred_element_type=F32)


def tn(left, right):
    return lax.dot_general(left, right, (((0,), (0,)), ((), ())), preferred_element_type=F32)


def whole(shape):
    zeros = (0,) * len(shape)
    return pl.BlockSpec(shape, lambda *_: zeros, pipeline_mode=pl.Buffered(1))


TOKEN = (8, 128)
RATE = 10e9


def run(
    body, name, pos, grid, inputs, outputs, us, mib, after=(), scratch=(), aliases={}, carry=()
):
    tokens = len(after)
    riders = len(carry)
    first = 1 + len(inputs)
    outs = first + tokens + riders
    last = outs + len(outputs)
    extra = 2 if carry else 1

    def wrapped(*refs):
        refs[last][...] = jnp.zeros(TOKEN, F32)
        if carry:
            added = [ref[...] for ref in refs[first + tokens : outs]]
            refs[last + 1][...] = sum(added[1:], added[0])
        body(*refs[:first], *refs[outs:last], *refs[last + extra :])

    whole_of = lambda a: whole(a.shape)
    out = pl.pallas_call(
        wrapped,
        grid_spec=pltpu.PrefetchScalarGridSpec(
            num_scalar_prefetch=1,
            grid=grid,
            in_specs=[spec for _, spec in inputs]
            + [pl.BlockSpec(memory_space=pl.ANY)] * tokens
            + [whole_of(a) for a in carry],
            out_specs=[spec for _, _, spec in outputs]
            + [whole(TOKEN)]
            + [whole_of(a) for a in carry[:1]],
            scratch_shapes=list(scratch),
        ),
        out_shape=[jax.ShapeDtypeStruct(shape, kind) for shape, kind, _ in outputs]
        + [jax.ShapeDtypeStruct(TOKEN, F32)]
        + [jax.ShapeDtypeStruct(a.shape, F32) for a in carry[:1]],
        compiler_params=pltpu.CompilerParams(
            dimension_semantics=("arbitrary",) * len(grid), vmem_limit_bytes=mib * MIB
        ),
        cost_estimate=pl.CostEstimate(
            flops=int(us * RATE), bytes_accessed=1000, transcendentals=0
        ),
        input_output_aliases=aliases,
        name=name,
    )(pos, *[array for array, _ in inputs], *after, *carry)
    if carry:
        return out[:-2], out[-2], out[-1]
    return out[:-1], out[-1]


def lane_half(shape):
    return lax.broadcasted_iota(jnp.int32, shape, 1) >= HEAD_DIM


def head_operands(upper, head, query, key, ones, mask):
    if head == 0:
        return jnp.where(upper, ones, query), jnp.where(upper, mask, key)
    return jnp.where(upper, query, ones), jnp.where(upper, key, mask)


def softmax_over_keys(scores):
    exponent = jnp.exp(scores - jnp.max(scores, axis=0, keepdims=True))
    return exponent * (1.0 / jnp.sum(exponent, axis=0, keepdims=True))


def norm(rows):
    center = jnp.mean(rows, axis=-1, keepdims=True)
    centered = rows - center
    variance = jnp.mean(centered * centered, axis=-1, keepdims=True)
    inverse = lax.rsqrt(variance + EPSILON)
    return centered * inverse, inverse


def norm_back(grad_result, scaled, inverse, gain):
    grad_scaled = grad_result * gain
    first_mean = jnp.mean(grad_scaled, axis=-1, keepdims=True)
    second_mean = jnp.mean(grad_scaled * scaled, axis=-1, keepdims=True)
    return inverse * (grad_scaled - first_mean - scaled * second_mean)


GROUP = HALF
GROUPS = WIDTH // GROUP


class Copies:
    def __init__(self, sems):
        self.sems, self.count, self.open = sems, 0, []

    def start(self, source, target):
        copy = pltpu.make_async_copy(source, target, self.sems.at[self.count])
        self.count += 1
        copy.start()
        self.open.append(copy)
        return copy

    def wait(self, copy):
        self.open.remove(copy)
        copy.wait()

    def finish(self):
        for copy in self.open:
            copy.wait()
        self.open = []


ATTEND_COPIES = 3 * GROUPS + 1 + GROUPS * 3 + 4


def attend_body(
    items,
    pos,
    own,
    other,
    mask,
    ones,
    w_qkv,
    query_bias,
    value_bias,
    w_out,
    out_bias,
    gain,
    shift,
    queries,
    keys,
    values,
    keep,
    scaled,
    inverse,
    qkv_weight,
    out_weight,
    qkv,
    kept,
    unit,
    sems,
):
    copies = Copies(sems)
    span = 2 * SLOTS
    loads = []
    for group in range(GROUPS):
        for part in range(3):
            cols = pl.ds(part * WIDTH + group * GROUP, GROUP)
            loads.append(copies.start(w_qkv.at[:, cols], qkv_weight.at[:, cols]))
    load_out = copies.start(w_out, out_weight)
    for item in range(items):
        kept[0, item * span : item * span + SLOTS, :] = own[item]
        kept[0, item * span + SLOTS : (item + 1) * span, :] = other[item]
    copies.start(kept.at[0], keep.at[0])
    rows = kept[0]
    upper = lane_half((span, PAIR))
    total = None
    for group in range(GROUPS):
        cols = slice(group * GROUP, (group + 1) * GROUP)
        for part in range(3):
            copies.wait(loads[3 * group + part])
            weight = qkv_weight[:, part * WIDTH + group * GROUP : part * WIDTH + (group + 1) * GROUP]
            made = nn(rows, weight)
            if part != 1:
                made = made + (query_bias, None, value_bias)[part][:, cols]
            qkv[part, :, cols] = made.astype(BF16)
        for part, target in enumerate((queries, keys, values)):
            copies.start(qkv.at[part, :, pl.ds(group * GROUP, GROUP)], target.at[:, pl.ds(group * GROUP, GROUP)])
        for item in range(items):
            at = slice(item * span, (item + 1) * span)
            for pair in range(GROUP // PAIR):
                place = slice(group * GROUP + pair * PAIR, group * GROUP + (pair + 1) * PAIR)
                query = qkv[0, at, place] * jnp.asarray(SCALE, BF16)
                key = qkv[1, at, place]
                value = qkv[2, at, place]
                heads = []
                for head in range(2):
                    query_h, key_h = head_operands(
                        upper, head, query, key, ones[...], mask[item]
                    )
                    probs = softmax_over_keys(nt(key_h, query_h))
                    heads.append(tn(probs.astype(BF16), value))
                kept[1, at, place] = jnp.where(upper, heads[1], heads[0]).astype(BF16)
    copies.start(kept.at[1], keep.at[1])
    copies.wait(load_out)
    branch = nn(kept[1], out_weight[...])
    unit_rows, inv = norm(rows.astype(F32) + (branch + out_bias[...]))
    unit[...] = unit_rows
    inverse[...] = inv
    copies.start(unit, scaled)
    kept[2] = (unit_rows * gain[...] + shift[...]).astype(BF16)
    copies.start(kept.at[2], keep.at[2])
    copies.finish()


def attend(pos, own, other, mask, ones, w_qkv, query_bias, value_bias, w_out, out_bias, gain, shift):
    items = own.shape[0]
    count = items * 2 * SLOTS
    shape = (count, WIDTH)
    anywhere = pl.BlockSpec(memory_space=pl.ANY)
    near = lambda a: (a, whole(a.shape))
    return run(
        functools.partial(attend_body, items),
        "attend",
        pos,
        (1,),
        [
            near(own),
            near(other),
            near(mask),
            near(ones),
            (w_qkv, anywhere),
            near(query_bias),
            near(value_bias),
            (w_out, anywhere),
            near(out_bias),
            near(gain),
            near(shift),
        ],
        [
            (shape, BF16, anywhere),
            (shape, BF16, anywhere),
            (shape, BF16, anywhere),
            ((3,) + shape, BF16, anywhere),
            (shape, F32, anywhere),
            ((count, 1), F32, whole((count, 1))),
        ],
        scratch=[
            pltpu.VMEM((WIDTH, 3 * WIDTH), BF16),
            pltpu.VMEM((WIDTH, WIDTH), BF16),
            pltpu.VMEM((3,) + shape, BF16),
            pltpu.VMEM((3,) + shape, BF16),
            pltpu.VMEM(shape, F32),
            pltpu.SemaphoreType.DMA((ATTEND_COPIES,)),
        ],
        us=10,
        mib=ATTEND_MIB,
    )


ATTEND_MIB = 24
FEED_MIB = 50
FEED_COPIES = 2 * CHUNKS + 3 + 12


def gelu_and_slope(upward):
    size = jnp.abs(upward)
    divisor = 1.0 + (0.3275911 * 0.7071067811865476) * size
    near = pl.reciprocal(divisor, approx=True)
    near = near * (2.0 - divisor * near)
    bell = jnp.exp(-0.5 * upward * upward)
    poly = 0.5 * 1.061405429 * near - 0.5 * 1.453152027
    poly = poly * near + 0.5 * 1.421413741
    poly = poly * near - 0.5 * 0.284496736
    poly = poly * near + 0.5 * 0.254829592
    tail = poly * near * bell
    phi = jnp.where(upward >= 0, 1.0 - tail, tail)
    return upward * phi, phi + upward * (bell * 0.3989422804014327)


def half_chunk(j, pos):
    return lax.rem(j + (1 - pos[0]) * (CHUNKS // 2), CHUNKS)


def feed_body(
    items,
    pos,
    keep,
    scaled,
    inverse,
    gain_one,
    shift_one,
    w_out,
    w_up,
    up_bias,
    w_down,
    down_bias,
    gain_two,
    shift_two,
    cot_own,
    cot_other,
    act_mine,
    send,
    out_own,
    out_other,
    up_theirs,
    up_mine,
    up_bias_grad,
    grad_first,
    branch_theirs,
    branch_mine,
    grad_attended,
    small,
    low_rows,
    unit_rows,
    out_weight,
    up_weight,
    down_weight,
    slope,
    sent,
    act,
    up_grad,
    first,
    branch,
    attended,
    sems,
):
    copies = Copies(sems)
    span = 2 * SLOTS
    half = CHUNKS // 2
    load_low = copies.start(keep.at[2], low_rows)
    load_up, load_down, places = [], [], []
    for chunk in range(CHUNKS):
        place = pl.multiple_of(half_chunk(chunk, pos) * CHUNK, CHUNK)
        places.append(place)
        load_up.append(copies.start(w_up.at[:, pl.ds(place, CHUNK)], up_weight.at[chunk]))
        load_down.append(copies.start(w_down.at[pl.ds(place, CHUNK), :], down_weight.at[chunk]))
    load_unit = copies.start(scaled, unit_rows)
    load_out = copies.start(w_out, out_weight)
    copies.wait(load_low)
    total = None
    for chunk in range(CHUNKS):
        copies.wait(load_up[chunk])
        upward = nn(low_rows[...], up_weight[chunk]) + up_bias[:, pl.ds(places[chunk], CHUNK)]
        active, steep = gelu_and_slope(upward)
        slope[chunk] = steep
        active = active.astype(BF16)
        if chunk < half:
            sent[:, chunk * CHUNK : (chunk + 1) * CHUNK] = active
        else:
            act[:, (chunk - half) * CHUNK : (chunk - half + 1) * CHUNK] = active
        copies.wait(load_down[chunk])
        part = nn(active, down_weight[chunk])
        total = part if total is None else total + part
    copies.start(act, act_mine)
    copies.wait(load_unit)
    normed = unit_rows[...] * gain_one[...] + shift_one[...]
    unit, inv = norm(normed + (total + down_bias[...]))
    result = (unit * gain_two[...] + shift_two[...]).astype(BF16)
    cots = []
    for item in range(items):
        out_own[item] = result[item * span : item * span + SLOTS]
        out_other[item] = result[item * span + SLOTS : (item + 1) * span]
        cots += [cot_own[item], cot_other[item]]
    cot = jnp.concatenate(cots, axis=0).astype(F32)
    grad = norm_back(cot, unit, inv, gain_two[...])
    low = grad.astype(BF16)
    sent[:, FF_HALF:] = low
    copies.start(sent, send)
    small[...] = jnp.zeros_like(small)
    small[3:4, :] = jnp.sum(low.astype(F32), axis=0, keepdims=True)
    small[4:5, :] = jnp.sum(cot * unit, axis=0, keepdims=True)
    small[5:6, :] = jnp.sum(cot, axis=0, keepdims=True)
    total = grad
    for chunk in range(CHUNKS):
        low = (nt(sent[:, FF_HALF:], down_weight[chunk]) * slope[chunk]).astype(BF16)
        up_grad[chunk] = low
        target = (up_theirs, up_mine)[chunk // half]
        copies.start(up_grad.at[chunk], target.at[:, pl.ds(chunk % half * CHUNK, CHUNK)])
        up_bias_grad[:, pl.ds(places[chunk], CHUNK)] = jnp.sum(
            low.astype(F32), axis=0, keepdims=True
        )
        total = total + nt(low, up_weight[chunk])
    unit = unit_rows[...]
    grad = norm_back(total, unit, inverse[...], gain_one[...])
    first[...] = grad
    copies.start(first, grad_first)
    branch[...] = grad.astype(BF16)
    mine = pl.multiple_of(pos[0] * HALF, HALF)
    theirs = pl.multiple_of((1 - pos[0]) * HALF, HALF)
    copies.start(branch.at[:, pl.ds(mine, HALF)], branch_mine)
    copies.start(branch.at[:, pl.ds(theirs, HALF)], branch_theirs)
    copies.wait(load_out)
    attended[...] = nt(branch[...], out_weight[...]).astype(BF16)
    copies.start(attended, grad_attended)
    small[0:1, :] = jnp.sum(branch[...].astype(F32), axis=0, keepdims=True)
    small[1:2, :] = jnp.sum(total * unit, axis=0, keepdims=True)
    small[2:3, :] = jnp.sum(total, axis=0, keepdims=True)
    copies.finish()


def feed(
    pos,
    keep,
    scaled,
    inverse,
    gain_one,
    shift_one,
    w_out,
    w_up,
    up_bias,
    w_down,
    down_bias,
    gain_two,
    shift_two,
    cot_own,
    cot_other,
):
    items = cot_own.shape[0]
    count = items * 2 * SLOTS
    shape = (count, WIDTH)
    anywhere = pl.BlockSpec(memory_space=pl.ANY)
    near = lambda a: (a, whole(a.shape))
    rows = whole(cot_own.shape)
    return run(
        functools.partial(feed_body, items),
        "feed",
        pos,
        (1,),
        [
            (keep, anywhere),
            (scaled, anywhere),
            near(inverse),
            near(gain_one),
            near(shift_one),
            (w_out, anywhere),
            (w_up, anywhere),
            near(up_bias),
            (w_down, anywhere),
            near(down_bias),
            near(gain_two),
            near(shift_two),
            near(cot_own),
            near(cot_other),
        ],
        [
            ((count, FF_HALF), BF16, anywhere),
            ((count, FF_HALF + WIDTH), BF16, anywhere),
            (cot_own.shape, BF16, rows),
            (cot_own.shape, BF16, rows),
            ((count, FF_HALF), BF16, anywhere),
            ((count, FF_HALF), BF16, anywhere),
            ((1, FF), F32, whole((1, FF))),
            (shape, F32, anywhere),
            ((count, HALF), BF16, anywhere),
            ((count, HALF), BF16, anywhere),
            (shape, BF16, anywhere),
            ((8, WIDTH), F32, whole((8, WIDTH))),
        ],
        scratch=[
            pltpu.VMEM(shape, BF16),
            pltpu.VMEM(shape, F32),
            pltpu.VMEM((WIDTH, WIDTH), BF16),
            pltpu.VMEM((CHUNKS, WIDTH, CHUNK), BF16),
            pltpu.VMEM((CHUNKS, CHUNK, WIDTH), BF16),
            pltpu.VMEM((CHUNKS, count, CHUNK), F32),
            pltpu.VMEM((count, FF_HALF + WIDTH), BF16),
            pltpu.VMEM((count, FF_HALF), BF16),
            pltpu.VMEM((CHUNKS, count, CHUNK), BF16),
            pltpu.VMEM(shape, F32),
            pltpu.VMEM(shape, BF16),
            pltpu.VMEM(shape, BF16),
            pltpu.SemaphoreType.DMA((FEED_COPIES,)),
        ],
        us=20,
        mib=FEED_MIB,
    )


def keep_rows(which, count, cols, place):
    return pl.BlockSpec((None, count, cols), lambda j, pos: (which, 0, place(j, pos)))


def attend_back_half(
    items, mask, ones, queries, keys, values, grad_attended, w_q, w_k, w_v, joined
):
    span = 2 * SLOTS
    upper = lane_half((span, PAIR))
    for item in range(items):
        at = slice(item * span, (item + 1) * span)
        for pair in range(HALF // PAIR):
            cols = slice(pair * PAIR, (pair + 1) * PAIR)
            query = queries[at, cols] * jnp.asarray(SCALE, BF16)
            key = keys[at, cols]
            value = values[at, cols]
            grad_out = grad_attended[at, cols]
            none = jnp.zeros_like(grad_out)
            grads = []
            for head in range(2):
                query_h, key_h = head_operands(
                    upper, head, query, key, ones[...], mask[item]
                )
                probs = softmax_over_keys(nt(key_h, query_h))
                if head == 0:
                    grad_h = jnp.where(upper, none, grad_out)
                else:
                    grad_h = jnp.where(upper, grad_out, none)
                grad_probs = nt(value, grad_h)
                inner = jnp.sum(probs * grad_probs, axis=0, keepdims=True)
                grad_scores = (probs * (grad_probs - inner)).astype(BF16)
                grads.append(
                    (
                        tn(grad_scores, key) * SCALE,
                        nn(grad_scores, query),
                        nn(probs.astype(BF16), grad_out),
                    )
                )
            for index in range(3):
                place = slice(index * HALF + pair * PAIR, index * HALF + (pair + 1) * PAIR)
                joined[at, place] = jnp.where(
                    upper, grads[1][index], grads[0][index]
                ).astype(BF16)
    parts = [joined[:, index * HALF : (index + 1) * HALF] for index in range(3)]
    sums = [jnp.sum(parts[index].astype(F32), axis=0, keepdims=True) for index in (0, 2)]
    total = nt(parts[0], w_q[...]) + nt(parts[1], w_k[...]) + nt(parts[2], w_v[...])
    return total, sums


def attend_back_body(items, pos, *refs):
    *ins, first, second, grad_first, small_in, up_bias, theirs, mine, own, other, small, total, joined = refs
    step = pl.program_id(0)
    span = 2 * SLOTS
    part, sums = attend_back_half(items, *ins, joined)

    @pl.when(step == 0)
    def _():
        theirs[:, : 3 * HALF] = joined[...]
        theirs[:, 3 * HALF :] = first[...]
        total[...] = grad_first[...] + part
        small[...] = jnp.zeros_like(small)
        small[0:8, :] = small_in[...]
        for index in range(FF // WIDTH):
            small[6 + index : 7 + index, :] = up_bias[:, index * WIDTH : (index + 1) * WIDTH]

    @pl.when(step == 1)
    def _():
        mine[:, : 3 * HALF] = joined[...]
        mine[:, 3 * HALF :] = second[...]
        for item in range(items):
            at = slice(item * span, item * span + SLOTS)
            own[item] = total[at, :] + part[at]
            at = slice(item * span + SLOTS, (item + 1) * span)
            other[item] = (total[at, :] + part[at]).astype(BF16)

    place = pl.multiple_of(lax.rem(step + 1 + pos[0], 2) * HALF, HALF)
    for index in range(2):
        small[10 + index : 11 + index, pl.ds(place, HALF)] = sums[index]


def attend_back(
    pos, mask, ones, queries, keys, values, grad_attended, w_qkv, first, second, grad_first, small, up_bias, after
):
    count = queries.shape[0]
    items = mask.shape[0]
    half = lambda j, pos: lax.rem(j + 1 + pos[0], 2)
    flat = pl.BlockSpec((count, HALF), lambda j, pos: (0, half(j, pos)))
    weight = lambda k: pl.BlockSpec((WIDTH, HALF), lambda j, pos: (0, 2 * k + half(j, pos)))
    joined = ((count, 4 * HALF), BF16, whole((count, 4 * HALF)))
    rows = whole((items, SLOTS, WIDTH))
    return run(
        functools.partial(attend_back_body, items),
        "attend_back",
        pos,
        (2,),
        [
            (mask, whole(mask.shape)),
            (ones, whole(ones.shape)),
            (queries, flat),
            (keys, flat),
            (values, flat),
            (grad_attended, flat),
            (w_qkv, weight(0)),
            (w_qkv, weight(1)),
            (w_qkv, weight(2)),
        ]
        + [(a, whole(a.shape)) for a in (first, second, grad_first, small, up_bias)],
        [
            joined,
            joined,
            ((items, SLOTS, WIDTH), F32, rows),
            ((items, SLOTS, WIDTH), BF16, rows),
            ((16, WIDTH), F32, whole((16, WIDTH))),
        ],
        after=after,
        scratch=[pltpu.VMEM((count, WIDTH), F32), pltpu.VMEM((count, 3 * HALF), BF16)],
        us=0.6,
        mib=32,
    )


TALL = HALF
LOW = TALL // 2
FAR, ACROSS, ALONG, OWN = 3, 2, 1, 0
PIECE = (TALL, WIDTH)


def quarter(pos, there):
    return pos[1] ^ (there >> 1), pos[2] ^ (there & 1)


def order_of(kind, step):
    first, second = (ACROSS, ALONG) if kind == "up" else (ALONG, ACROSS)
    return jnp.where(step == 0, FAR, jnp.where(step == 1, first, jnp.where(step == 2, second, OWN)))


def gradient_body(kind, block, outs, pos, *refs):
    ins, outs = refs[:-outs], refs[-outs:]
    step = pl.program_id(0)
    value = block(quarter(pos, order_of(kind, step))[1], *ins).astype(BF16)
    if kind == "mixed":
        targets = [None, outs[2], outs[3], outs[4]]
    else:
        targets = [outs[0].at[0], outs[0].at[1], outs[1], outs[2]]
    for index, target in enumerate(targets):

        @pl.when(step == index)
        def _(target=target):
            if target is None:
                outs[0][...] = value[:LOW]
                outs[1][...] = value[LOW:]
            else:
                target[...] = value


def plain_block(along, left_a, left_b, right_a, right_b):
    return tn(left_a[...], right_a[...]) + tn(left_b[...], right_b[...])


def mixed_block(along, rows_a, rows_b, att_a, att_b, right_a, right_b):
    left_a = jnp.where(along == 0, rows_a[...], att_a[...])
    left_b = jnp.where(along == 0, rows_b[...], att_b[...])
    return jnp.concatenate(
        [
            tn(rows_a[...], right_a[:, :HALF]) + tn(rows_b[...], right_b[:, :HALF]),
            tn(left_a, right_a[:, HALF:]) + tn(left_b, right_b[:, HALF:]),
        ],
        axis=1,
    )


def gradient(kind, pos, operands, after):
    count = operands[-1].shape[0]
    across = lambda j, pos: quarter(pos, order_of(kind, j))[0]
    along = lambda j, pos: quarter(pos, order_of(kind, j))[1]
    block = plain_block
    if kind == "down":
        lefts = pl.BlockSpec(
            (count, TALL), lambda j, pos: (0, 2 * across(j, pos) + along(j, pos))
        )
        rights = pl.BlockSpec((count, WIDTH), lambda j, pos: (0, FF_HALF // WIDTH))
        specs = [lefts, lefts, rights, rights]
    else:
        rights = pl.BlockSpec((count, WIDTH), lambda j, pos: (0, along(j, pos)))
        if kind == "up":
            lefts = keep_rows(2, count, TALL, across)
            specs = [lefts, lefts, rights, rights]
        else:
            rows, att = keep_rows(0, count, TALL, across), keep_rows(1, count, TALL, across)
            specs = [rows, rows, att, att, rights, rights]
            block = mixed_block
    if kind == "mixed":
        shapes = [(LOW, WIDTH)] * 2 + [PIECE] * 3
    else:
        shapes = [(2,) + PIECE] + [PIECE] * 2
    return run(
        functools.partial(gradient_body, kind, block, len(shapes)),
        kind + "_gradient",
        pos,
        (4,),
        list(zip(operands, specs)),
        [(shape, BF16, whole(shape)) for shape in shapes],
        after=after,
        us=0.3,
        mib=20,
    )


def sum_body(share, pos, *refs):
    ins = refs[:-3] if share else refs[:-1]
    total = ins[0][...].astype(F32)
    for ref in ins[1:]:
        total = total + ref[...].astype(F32)
    if not share:
        refs[-1][...] = total.astype(BF16)
        return
    held = refs[-1]
    held[...] = total
    for turn in range(2):
        first = pl.multiple_of((pos[3] ^ turn) * LOW, LOW)
        refs[turn - 3][...] = held[pl.ds(first, LOW), :].astype(BF16)


def sum_of(pos, arrays, after, share=False, carry=(), us=1):
    shape = arrays[0].shape
    item = lambda index: pl.BlockSpec((None,) + PIECE, lambda *_: (index, 0, 0))
    shapes = [(LOW, WIDTH)] * 2 if share else [shape]
    out, *more = run(
        functools.partial(sum_body, share),
        "sum_shares" if share else "sum_of",
        pos,
        (1,),
        [
            (a[0], item(a[1])) if isinstance(a, tuple) else (a, whole(shape))
            for a in arrays
        ],
        [(shape, BF16, whole(shape)) for shape in shapes],
        after=after,
        scratch=[pltpu.VMEM(shape, F32)] if share else [],
        us=us,
        mib=8,
        carry=carry,
    )
    return (out if share else out[0]), *more


def sides_body(pos, along, across, low, high, along_out, across_out):
    along_out[:LOW, :] = along[:LOW, :]
    along_out[LOW:, :] = (along[LOW:, :].astype(F32) + high[...].astype(F32)).astype(BF16)
    across_out[:LOW, :] = (across[:LOW, :].astype(F32) + low[...].astype(F32)).astype(BF16)
    across_out[LOW:, :] = across[LOW:, :]


def sum_sides(pos, along, across, low, high, after, carry=()):
    return run(
        sides_body,
        "sum_sides",
        pos,
        (1,),
        [(a, whole(a.shape)) for a in (along, across, low, high)],
        [(PIECE, BF16, whole(PIECE))] * 2,
        after=after,
        carry=carry,
        us=0.1,
        mib=8,
    )


def split_body(pos, own, first, second, low, high, packed):
    low[...] = first[:LOW, :]
    high[...] = second[LOW:, :]
    for index, ref in enumerate((own, first, second)):
        packed[index] = ref[...]


def split(pos, own, first, second, after):
    half = (LOW, WIDTH)
    return run(
        split_body,
        "split",
        pos,
        (1,),
        [(a, whole(PIECE)) for a in (own, first, second)],
        [(half, BF16, whole(half))] * 2 + [((3,) + PIECE, BF16, whole((3,) + PIECE))],
        after=after,
        us=1,
        mib=10,
    )


def pack_body(pos, *refs):
    for index, ref in enumerate(refs[:-1]):
        refs[-1][index] = ref[...]


def pack(pos, pieces, after):
    shape = (len(pieces),) + PIECE
    out, token = run(
        pack_body,
        "pack",
        pos,
        (1,),
        [(a, whole(PIECE)) for a in pieces],
        [(shape, BF16, whole(shape))],
        after=after,
        us=0.1,
        mib=12,
    )
    return out[0], token


def stack_halves(pos, low, high, after):
    half = (LOW, WIDTH)
    out, token = run(
        pack_body,
        "stack_halves",
        pos,
        (1,),
        [(low, whole(half)), (high, whole(half))],
        [((2,) + half, BF16, whole((2,) + half))],
        after=after,
        us=0.1,
        mib=6,
    )
    return out[0], token


def join_body(pos, mine, theirs, out):
    for turn, ref in enumerate((mine, theirs)):
        first = pl.multiple_of((pos[3] ^ turn) * LOW, LOW)
        out[pl.ds(first, LOW), :] = ref[...]


def join_shares(pos, shares, after, carry=()):
    out, *more = run(
        join_body,
        "join_shares",
        pos,
        (1,),
        [(a, whole(a.shape)) for a in shares],
        [(PIECE, BF16, whole(PIECE))],
        after=after,
        us=0.1,
        mib=6,
        carry=carry,
    )
    return out[0], *more


def place_body(kind, entries, outs, pos, *refs):
    sources = iter(refs)
    pieces = []
    for _, _, _, _, index in entries:
        if not index:
            ref = next(sources)
        pieces.append(ref if index is None else ref.at[index])
    targets = refs[len(refs) - 4 - outs : len(refs) - 4]
    taken, given, in_sems, out_sems = refs[-4:]
    fetches = []
    for index, (rows, *_) in enumerate(entries):
        fetch = pltpu.make_async_copy(
            pieces[index], taken.at[index, pl.ds(0, rows)], in_sems.at[index]
        )
        fetch.start()
        fetches.append(fetch)

    def sends(index):
        rows, theirs, there, start, _ = entries[index]
        half = pos[0] ^ theirs
        across, along = quarter(pos, there)
        source = given.at[index]
        if kind == "down":
            first = pl.multiple_of((4 * half + 2 * across + along) * TALL + start, LOW)
            yield None, source.at[pl.ds(0, rows)], targets[0].at[pl.ds(first, rows)], 0
            return
        first = pl.multiple_of(across * TALL + start, LOW)
        if kind == "up":
            column = pl.multiple_of((2 * half + along) * WIDTH, WIDTH)
            target = targets[0].at[pl.ds(first, rows), pl.ds(column, WIDTH)]
            yield None, source.at[pl.ds(0, rows)], target, 0
            return
        for part in range(2):
            source_part = source.at[pl.ds(0, rows), pl.ds(part * HALF, HALF)]
            column = pl.multiple_of(jnp.minimum(2 * along + part, 2) * WIDTH + half * HALF, HALF)
            target = targets[0].at[pl.ds(first, rows), pl.ds(column, HALF)]
            if part == 0:
                yield None, source_part, target, 0
            else:
                yield along == 0, source_part, target, 1
                column = pl.multiple_of(half * HALF, HALF)
                target = targets[1].at[pl.ds(first, rows), pl.ds(column, HALF)]
                yield along == 1, source_part, target, 1

    def each(index, act):
        for condition, source, target, sem in sends(index):
            copy = pltpu.make_async_copy(source, target, out_sems.at[index, sem])
            if condition is None:
                act(copy)
            else:

                @pl.when(condition)
                def _(copy=copy):
                    act(copy)

    for index, (rows, *_) in enumerate(entries):
        fetches[index].wait()
        given[index, :rows, :] = taken[index, :rows, :].astype(F32)
        each(index, lambda copy: copy.start())
    for index in range(len(entries)):
        each(index, lambda copy: copy.wait())


def place(kind, pos, pieces, before, after):
    pieces = [piece if len(piece) == 5 else piece + (None,) for piece in pieces]
    entries = tuple((p.shape[-2],) + tuple(more) for p, *more in pieces)
    shapes = {
        "down": [(FF, WIDTH)],
        "up": [(WIDTH, FF)],
        "mixed": [(WIDTH, 3 * WIDTH), (WIDTH, WIDTH)],
    }[kind]
    anywhere = pl.BlockSpec(memory_space=pl.ANY)
    arrays = [p for p, *_, index in pieces if not index]
    ins = [(a, anywhere) for a in arrays + list(before)]
    count = len(entries)
    return run(
        functools.partial(place_body, kind, entries, len(shapes)),
        "place_" + kind,
        pos,
        (1,),
        ins,
        [(shape, F32, anywhere) for shape in shapes],
        after=after,
        scratch=[
            pltpu.VMEM((count, TALL, WIDTH), BF16),
            pltpu.VMEM((count, TALL, WIDTH), F32),
            pltpu.SemaphoreType.DMA((count,)),
            pltpu.SemaphoreType.DMA((count, 2)),
        ],
        aliases={1 + len(arrays) + index: index for index in range(len(before))},
        us=0.02,
        mib=22,
    )


def place_rows_body(pos, own, got, own_grad, got_grad, out, grad):
    @pl.when(pl.program_id(0) == 0)
    def _():
        out[...] = own[...]
        grad[...] = own_grad[...]

    @pl.when(pl.program_id(0) == 1)
    def _():
        out[...] = got[...]
        grad[...] = got_grad[...].astype(F32)


def place_rows(pos, own, got, own_grad, got_grad, after):
    items = own.shape[0]
    spec = pl.BlockSpec(own.shape, lambda step, pos: (pos[1] ^ step, 0, 0))
    shape = (2 * items,) + own.shape[1:]
    return run(
        place_rows_body,
        "place_rows",
        pos,
        (2,),
        [(a, whole(own.shape)) for a in (own, got, own_grad, got_grad)],
        [(shape, BF16, spec), (shape, F32, spec)],
        after=after,
        us=0.02,
        mib=10,
    )


def local(
    batch,
    tokens,
    caption_lengths,
    region_mask,
    w_qkv,
    query_bias,
    value_bias,
    w_out,
    out_bias,
    w_up,
    up_bias,
    w_down,
    down_bias,
    gain_one,
    shift_one,
    gain_two,
    shift_two,
    cotangent,
):
    swap_core = [(i, i ^ 1) for i in range(batch)]
    swap_along = [(i, i ^ 2) for i in range(batch)]
    swap_across = [(0, 1), (1, 0)]
    line = [[4 * k + i for k in range(batch // 4)] for i in range(4)]
    same_core = [[2 * k + i for k in range(batch // 2)] for i in range(2)]
    core = lambda a: lax.ppermute(a, "batch", swap_core)
    along = lambda a: lax.ppermute(a, "batch", swap_along)
    across = lambda a: lax.ppermute(a, "mod", swap_across)

    place_y = lax.axis_index("mod")
    place_b = lax.axis_index("batch")
    pos = jnp.stack([place_b % 2, place_y, (place_b // 2) % 2, (place_b // 4) % 2]).astype(jnp.int32)
    items = tokens.shape[0] // 2
    mine = place_y * items
    rest = (1 - place_y) * items
    rows = lambda a, start: lax.dynamic_slice_in_dim(a, start, items, axis=0)

    other_tokens = across(rows(tokens, rest))
    other_cot = across(rows(cotangent, rest))
    own_tokens = rows(tokens, mine)
    own_cot = rows(cotangent, mine)

    slot = lax.broadcasted_iota(jnp.int32, (items, SLOTS), 1)
    text = slot < rows(caption_lengths, mine)[:, None]
    region = rows(region_mask, mine) > 0
    valid = jnp.concatenate(
        [jnp.where(place_y == 0, text, region), jnp.where(place_y == 0, region, text)], axis=1
    )
    lane = lax.broadcasted_iota(jnp.int32, (1, 1, PAIR), 2) % HEAD_DIM == 0
    mask = jnp.where(lane & ~valid[:, :, None], MASKED, 0.0).astype(BF16)
    ones = jnp.where(
        lax.broadcasted_iota(jnp.int32, (2 * SLOTS, PAIR), 1) % HEAD_DIM == 0, 1.0, 0.0
    ).astype(BF16)
    line_of = lambda a: a.reshape(1, -1)

    (queries, keys, values, keep, scaled, inverse), _ = attend(
        pos,
        own_tokens,
        other_tokens,
        mask,
        ones,
        w_qkv,
        line_of(query_bias),
        line_of(value_bias),
        w_out,
        line_of(out_bias),
        line_of(gain_one),
        line_of(shift_one),
    )
    (
        (
            act_mine,
            send,
            out_own,
            out_other,
            up_theirs,
            up_mine,
            up_bias_grad,
            grad_first,
            branch_theirs,
            branch_mine,
            grad_attended,
            small,
        ),
        done,
    ) = feed(
        pos,
        keep,
        scaled,
        inverse,
        line_of(gain_one),
        line_of(shift_one),
        w_out,
        w_up,
        line_of(up_bias),
        w_down,
        line_of(down_bias),
        line_of(gain_two),
        line_of(shift_two),
        own_cot,
        other_cot,
    )
    send_got, keep_got, up_got = core(send), core(keep), core(up_theirs)
    out_got = across(out_other)
    by_shares = batch == 16
    near = lambda a: lax.ppermute(a, "batch", [(i, i ^ 4) for i in range(batch)])
    wide = lambda a: lax.ppermute(a, "batch", [(i, i ^ 8) for i in range(batch)])

    def line_sum(piece, turn):
        return lax.psum(piece, "batch", axis_index_groups=line[turn:] + line[:turn])

    hops = [across]
    bit = 2
    while bit < batch:
        hops.append(
            lambda a, bit=bit: lax.ppermute(a, "batch", [(i, i ^ bit) for i in range(batch)])
        )
        bit *= 2
    hops.append(core)

    def ride(kernel, *args, **more):
        nonlocal small, got, riding
        if not riding:
            return kernel(*args, **more)
        out, done, small = kernel(
            *args, **more, carry=(small,) if got is None else (small, got)
        )
        got = hops.pop(0)(small) if hops else None
        return out, done

    (down_pair, down_across, down_own), done = gradient(
        "down", pos, (act_mine, send_got, send, send_got), (done,)
    )
    down_pair = along(down_pair)
    (up_pair, up_along, up_own), done = gradient(
        "up", pos, (keep, keep_got, up_mine, up_got), (done, out_got)
    )
    up_pair = across(up_pair)
    (joint_theirs, joint_mine, grad_own, grad_other, small), done = attend_back(
        pos,
        mask,
        ones,
        queries,
        keys,
        values,
        grad_attended,
        w_qkv,
        branch_theirs,
        branch_mine,
        grad_first,
        small,
        up_bias_grad,
        (done,),
    )
    joint_got = core(joint_theirs)
    down_across, done = sum_of(pos, (down_across, (down_pair, 0)), (done,))
    down_across = across(down_across)
    up_along, done = sum_of(pos, (up_along, (up_pair, 0)), (done,))
    up_along = along(up_along)
    (mixed_low, mixed_high, mixed_along, mixed_across, mixed_own), done = gradient(
        "mixed", pos, (keep, keep_got, keep, keep_got, joint_mine, joint_got), (done,)
    )
    mixed_low, mixed_high = along(mixed_low), across(mixed_high)
    got, riding = None, False

    def halves(arrays, done, turn):
        parts, done = ride(sum_of, pos, arrays, (done,), share=by_shares, us=0.1)
        if by_shares:
            return (parts[0], near(parts[1])), done
        return line_sum(parts, turn), done

    def widen(parts, after):
        if not by_shares:
            return parts, after[0]
        half, done = ride(sum_of, pos, parts, after, us=0.1)
        return (half, wide(half)), done

    def narrow(parts, after):
        if not by_shares:
            return parts, after[0]
        half, done = ride(sum_of, pos, parts, after, us=0.1)
        return (half, near(half)), done

    def joined(parts, after):
        return ride(join_shares, pos, parts, after) if by_shares else (parts, after[0])

    down_sum, done = halves((down_own, (down_pair, 1), down_across), done, 0)
    up_sum, done = halves((up_own, (up_pair, 1), up_along), done, 1)
    (mixed_along, mixed_across), done = ride(
        sum_sides, pos, mixed_along, mixed_across, mixed_low, mixed_high, (done,)
    )
    mixed_along, mixed_across = along(mixed_along), across(mixed_across)
    down_sum, done = widen(down_sum, (done,))
    riding = True
    down_sum, done = narrow(down_sum, (done,))
    up_sum, done = widen(up_sum, (done,))
    mixed_sum, done = halves((mixed_own, mixed_along, mixed_across), done, 2)
    grad_got = across(grad_other)
    down_sum, done = joined(down_sum, (done, grad_got))
    down_x, down_y = along(down_sum), across(down_sum)
    up_sum, done = narrow(up_sum, (done,))
    mixed_sum, done = widen(mixed_sum, (done, down_x, down_y))
    up_sum, done = joined(up_sum, (done,))
    up_x, up_y = along(up_sum), across(up_sum)
    mixed_sum, done = narrow(mixed_sum, (done, up_x, up_y))
    while hops or got is not None:
        small = small + (hops.pop(0)(small) if got is None else got)
        got = None
    vectors = [small[index] for index in range(12)]
    vectors[6] = small[6:10].reshape(FF)
    seen = tuple(vectors[index] for index in (0, 1, 2, 3, 4, 5, 6, 10, 11))
    down_pack, done = pack(pos, (down_sum, down_x, down_y, across(down_x)), (done,))
    mixed_sum, done = joined(mixed_sum, (done,))
    mixed_x, mixed_y = along(mixed_sum), across(mixed_sum)
    up_pack, done = pack(pos, (up_sum, up_x, up_y, along(up_y)), (done,))
    (layer_output, input_grad), done = place_rows(
        pos, out_own, out_got, grad_own, grad_got, (done,)
    )
    def both(pieces):
        return [(p, 0, there, start) for p, there, start in pieces] + [
            (core(p), 1, there, start) for p, there, start in pieces
        ]

    def packed(pieces):
        places = list(enumerate((OWN, ALONG, ACROSS, FAR)))[: pieces.shape[0]]
        return [
            (array, theirs, there, 0, index)
            for theirs, array in enumerate((pieces, core(pieces)))
            for index, there in places
        ]

    (grad_down,), done = place(
        "down",
        pos,
        packed(down_pack),
        (),
        (done,),
    )
    (grad_up,), done = place(
        "up",
        pos,
        packed(up_pack),
        (),
        (done,),
    )
    (mixed_low, mixed_high, mixed_pack), done = split(pos, mixed_sum, mixed_x, mixed_y, (done,))
    mixed_low, mixed_high = across(mixed_low), along(mixed_high)
    partial, done = place(
        "mixed",
        pos,
        packed(mixed_pack),
        (),
        (done,),
    )
    last, done = stack_halves(pos, mixed_low, mixed_high, (done,) + seen)
    ends = [
        (array, theirs, FAR, start, index)
        for theirs, array in enumerate((last, core(last)))
        for index, start in enumerate((0, LOW))
    ]
    (grad_qkv, grad_out), done = place("mixed", pos, ends, partial, (done,))
    return (
        layer_output,
        input_grad,
        grad_qkv,
        vectors[10],
        vectors[11],
        grad_out,
        vectors[0],
        grad_up,
        vectors[6],
        grad_down,
        vectors[3],
        vectors[1],
        vectors[2],
        vectors[4],
        vectors[5],
    )


def solution(mesh):
    rows = P("batch", "mod", None)
    return jax.shard_map(
        functools.partial(local, mesh.shape["batch"]),
        mesh=mesh,
        in_specs=(rows, P("batch"), P("batch", None)) + (P(),) * 13 + (rows,),
        out_specs=(rows, rows) + (P(),) * 13,
        check_vma=False,
    )
```

```python
import functools

import jax
import jax.numpy as jnp
from jax import lax
from jax.experimental import pallas as pl
from jax.experimental.pallas import tpu as pltpu
from jax.sharding import PartitionSpec as P

HEADS = 12
HEAD_DIM = 64
WIDTH = 768
FF = 3072
SLOTS = 128
EPSILON = 1e-12
PAIR = 2 * HEAD_DIM
HALF = WIDTH // 2
FF_HALF = FF // 2
CHUNK = 768
CHUNKS = FF // CHUNK
MASKED = -1e30
SCALE = HEAD_DIM ** (-0.5)
MIB = 1 << 20

BF16 = jnp.bfloat16
F32 = jnp.float32


def nn(left, right):
    return lax.dot_general(left, right, (((1,), (0,)), ((), ())), preferred_element_type=F32)


def nt(left, right):
    return lax.dot_general(left, right, (((1,), (1,)), ((), ())), preferred_element_type=F32)


def tn(left, right):
    return lax.dot_general(left, right, (((0,), (0,)), ((), ())), preferred_element_type=F32)


def whole(shape):
    zeros = (0,) * len(shape)
    return pl.BlockSpec(shape, lambda *_: zeros, pipeline_mode=pl.Buffered(1))


TOKEN = (8, 128)
RATE = 10e9


def run(
    body, name, pos, grid, inputs, outputs, us, mib, after=(), scratch=(), aliases={}, carry=()
):
    tokens = len(after)
    riders = len(carry)
    first = 1 + len(inputs)
    outs = first + tokens + riders
    last = outs + len(outputs)
    extra = 2 if carry else 1

    def wrapped(*refs):
        refs[last][...] = jnp.zeros(TOKEN, F32)
        if carry:
            added = [ref[...] for ref in refs[first + tokens : outs]]
            refs[last + 1][...] = sum(added[1:], added[0])
        body(*refs[:first], *refs[outs:last], *refs[last + extra :])

    whole_of = lambda a: whole(a.shape)
    out = pl.pallas_call(
        wrapped,
        grid_spec=pltpu.PrefetchScalarGridSpec(
            num_scalar_prefetch=1,
            grid=grid,
            in_specs=[spec for _, spec in inputs]
            + [pl.BlockSpec(memory_space=pl.ANY)] * tokens
            + [whole_of(a) for a in carry],
            out_specs=[spec for _, _, spec in outputs]
            + [whole(TOKEN)]
            + [whole_of(a) for a in carry[:1]],
            scratch_shapes=list(scratch),
        ),
        out_shape=[jax.ShapeDtypeStruct(shape, kind) for shape, kind, _ in outputs]
        + [jax.ShapeDtypeStruct(TOKEN, F32)]
        + [jax.ShapeDtypeStruct(a.shape, F32) for a in carry[:1]],
        compiler_params=pltpu.CompilerParams(
            dimension_semantics=("arbitrary",) * len(grid), vmem_limit_bytes=mib * MIB
        ),
        cost_estimate=pl.CostEstimate(
            flops=int(us * RATE), bytes_accessed=1000, transcendentals=0
        ),
        input_output_aliases=aliases,
        name=name,
    )(pos, *[array for array, _ in inputs], *after, *carry)
    if carry:
        return out[:-2], out[-2], out[-1]
    return out[:-1], out[-1]


def lane_half(shape):
    return lax.broadcasted_iota(jnp.int32, shape, 1) >= HEAD_DIM


def head_operands(upper, head, query, key, ones, mask):
    if head == 0:
        return jnp.where(upper, ones, query), jnp.where(upper, mask, key)
    return jnp.where(upper, query, ones), jnp.where(upper, key, mask)


def softmax_over_keys(scores):
    exponent = jnp.exp(scores - jnp.max(scores, axis=0, keepdims=True))
    return exponent * (1.0 / jnp.sum(exponent, axis=0, keepdims=True))


def norm(rows):
    center = jnp.mean(rows, axis=-1, keepdims=True)
    centered = rows - center
    variance = jnp.mean(centered * centered, axis=-1, keepdims=True)
    inverse = lax.rsqrt(variance + EPSILON)
    return centered * inverse, inverse


def norm_back(grad_result, scaled, inverse, gain):
    grad_scaled = grad_result * gain
    first_mean = jnp.mean(grad_scaled, axis=-1, keepdims=True)
    second_mean = jnp.mean(grad_scaled * scaled, axis=-1, keepdims=True)
    return inverse * (grad_scaled - first_mean - scaled * second_mean)


GROUP = HALF
GROUPS = WIDTH // GROUP


class Copies:
    def __init__(self, sems):
        self.sems, self.count, self.open = sems, 0, []

    def start(self, source, target):
        copy = pltpu.make_async_copy(source, target, self.sems.at[self.count])
        self.count += 1
        copy.start()
        self.open.append(copy)
        return copy

    def wait(self, copy):
        self.open.remove(copy)
        copy.wait()

    def finish(self):
        for copy in self.open:
            copy.wait()
        self.open = []


ATTEND_COPIES = 3 * GROUPS + 1 + GROUPS * 3 + 4


def attend_body(
    items,
    pos,
    own,
    other,
    mask,
    ones,
    w_qkv,
    query_bias,
    value_bias,
    w_out,
    out_bias,
    gain,
    shift,
    queries,
    keys,
    values,
    keep,
    scaled,
    inverse,
    qkv_weight,
    out_weight,
    qkv,
    kept,
    unit,
    sems,
):
    copies = Copies(sems)
    span = 2 * SLOTS
    loads = []
    for group in range(GROUPS):
        for part in range(3):
            cols = pl.ds(part * WIDTH + group * GROUP, GROUP)
            loads.append(copies.start(w_qkv.at[:, cols], qkv_weight.at[:, cols]))
    load_out = copies.start(w_out, out_weight)
    for item in range(items):
        kept[0, item * span : item * span + SLOTS, :] = own[item]
        kept[0, item * span + SLOTS : (item + 1) * span, :] = other[item]
    copies.start(kept.at[0], keep.at[0])
    rows = kept[0]
    upper = lane_half((span, PAIR))
    total = None
    for group in range(GROUPS):
        cols = slice(group * GROUP, (group + 1) * GROUP)
        for part in range(3):
            copies.wait(loads[3 * group + part])
            weight = qkv_weight[:, part * WIDTH + group * GROUP : part * WIDTH + (group + 1) * GROUP]
            made = nn(rows, weight)
            if part != 1:
                made = made + (query_bias, None, value_bias)[part][:, cols]
            qkv[part, :, cols] = made.astype(BF16)
        for part, target in enumerate((queries, keys, values)):
            copies.start(qkv.at[part, :, pl.ds(group * GROUP, GROUP)], target.at[:, pl.ds(group * GROUP, GROUP)])
        for item in range(items):
            at = slice(item * span, (item + 1) * span)
            for pair in range(GROUP // PAIR):
                place = slice(group * GROUP + pair * PAIR, group * GROUP + (pair + 1) * PAIR)
                query = qkv[0, at, place] * jnp.asarray(SCALE, BF16)
                key = qkv[1, at, place]
                value = qkv[2, at, place]
                heads = []
                for head in range(2):
                    query_h, key_h = head_operands(
                        upper, head, query, key, ones[...], mask[item]
                    )
                    probs = softmax_over_keys(nt(key_h, query_h))
                    heads.append(tn(probs.astype(BF16), value))
                kept[1, at, place] = jnp.where(upper, heads[1], heads[0]).astype(BF16)
    copies.start(kept.at[1], keep.at[1])
    copies.wait(load_out)
    branch = nn(kept[1], out_weight[...])
    unit_rows, inv = norm(rows.astype(F32) + (branch + out_bias[...]))
    unit[...] = unit_rows
    inverse[...] = inv
    copies.start(unit, scaled)
    kept[2] = (unit_rows * gain[...] + shift[...]).astype(BF16)
    copies.start(kept.at[2], keep.at[2])
    copies.finish()


def attend(pos, own, other, mask, ones, w_qkv, query_bias, value_bias, w_out, out_bias, gain, shift):
    items = own.shape[0]
    count = items * 2 * SLOTS
    shape = (count, WIDTH)
    anywhere = pl.BlockSpec(memory_space=pl.ANY)
    near = lambda a: (a, whole(a.shape))
    return run(
        functools.partial(attend_body, items),
        "attend",
        pos,
        (1,),
        [
            near(own),
            near(other),
            near(mask),
            near(ones),
            (w_qkv, anywhere),
            near(query_bias),
            near(value_bias),
            (w_out, anywhere),
            near(out_bias),
            near(gain),
            near(shift),
        ],
        [
            (shape, BF16, anywhere),
            (shape, BF16, anywhere),
            (shape, BF16, anywhere),
            ((3,) + shape, BF16, anywhere),
            (shape, F32, anywhere),
            ((count, 1), F32, whole((count, 1))),
        ],
        scratch=[
            pltpu.VMEM((WIDTH, 3 * WIDTH), BF16),
            pltpu.VMEM((WIDTH, WIDTH), BF16),
            pltpu.VMEM((3,) + shape, BF16),
            pltpu.VMEM((3,) + shape, BF16),
            pltpu.VMEM(shape, F32),
            pltpu.SemaphoreType.DMA((ATTEND_COPIES,)),
        ],
        us=10,
        mib=ATTEND_MIB,
    )


ATTEND_MIB = 24
FEED_MIB = 50
FEED_COPIES = 2 * CHUNKS + 3 + 12


def gelu_and_slope(upward):
    size = jnp.abs(upward)
    divisor = 1.0 + (0.3275911 * 0.7071067811865476) * size
    near = pl.reciprocal(divisor, approx=True)
    near = near * (2.0 - divisor * near)
    bell = jnp.exp(-0.5 * upward * upward)
    poly = 0.5 * 1.061405429 * near - 0.5 * 1.453152027
    poly = poly * near + 0.5 * 1.421413741
    poly = poly * near - 0.5 * 0.284496736
    poly = poly * near + 0.5 * 0.254829592
    tail = poly * near * bell
    phi = jnp.where(upward >= 0, 1.0 - tail, tail)
    return upward * phi, phi + upward * (bell * 0.3989422804014327)


def half_chunk(j, pos):
    return lax.rem(j + (1 - pos[0]) * (CHUNKS // 2), CHUNKS)


def feed_body(
    items,
    pos,
    keep,
    scaled,
    inverse,
    gain_one,
    shift_one,
    w_out,
    w_up,
    up_bias,
    w_down,
    down_bias,
    gain_two,
    shift_two,
    cot_own,
    cot_other,
    act_mine,
    send,
    out_own,
    out_other,
    up_theirs,
    up_mine,
    up_bias_grad,
    grad_first,
    branch_theirs,
    branch_mine,
    grad_attended,
    small,
    low_rows,
    unit_rows,
    out_weight,
    up_weight,
    down_weight,
    slope,
    sent,
    act,
    up_grad,
    first,
    branch,
    attended,
    sems,
):
    copies = Copies(sems)
    span = 2 * SLOTS
    half = CHUNKS // 2
    load_low = copies.start(keep.at[2], low_rows)
    load_up, load_down, places = [], [], []
    for chunk in range(CHUNKS):
        place = pl.multiple_of(half_chunk(chunk, pos) * CHUNK, CHUNK)
        places.append(place)
        load_up.append(copies.start(w_up.at[:, pl.ds(place, CHUNK)], up_weight.at[chunk]))
        load_down.append(copies.start(w_down.at[pl.ds(place, CHUNK), :], down_weight.at[chunk]))
    load_unit = copies.start(scaled, unit_rows)
    load_out = copies.start(w_out, out_weight)
    copies.wait(load_low)
    total = None
    for chunk in range(CHUNKS):
        copies.wait(load_up[chunk])
        upward = nn(low_rows[...], up_weight[chunk]) + up_bias[:, pl.ds(places[chunk], CHUNK)]
        active, steep = gelu_and_slope(upward)
        slope[chunk] = steep
        active = active.astype(BF16)
        if chunk < half:
            sent[:, chunk * CHUNK : (chunk + 1) * CHUNK] = active
        else:
            act[:, (chunk - half) * CHUNK : (chunk - half + 1) * CHUNK] = active
        copies.wait(load_down[chunk])
        part = nn(active, down_weight[chunk])
        total = part if total is None else total + part
    copies.start(act, act_mine)
    copies.wait(load_unit)
    normed = unit_rows[...] * gain_one[...] + shift_one[...]
    unit, inv = norm(normed + (total + down_bias[...]))
    result = (unit * gain_two[...] + shift_two[...]).astype(BF16)
    cots = []
    for item in range(items):
        out_own[item] = result[item * span : item * span + SLOTS]
        out_other[item] = result[item * span + SLOTS : (item + 1) * span]
        cots += [cot_own[item], cot_other[item]]
    cot = jnp.concatenate(cots, axis=0).astype(F32)
    grad = norm_back(cot, unit, inv, gain_two[...])
    low = grad.astype(BF16)
    sent[:, FF_HALF:] = low
    copies.start(sent, send)
    small[...] = jnp.zeros_like(small)
    small[3:4, :] = jnp.sum(low.astype(F32), axis=0, keepdims=True)
    small[4:5, :] = jnp.sum(cot * unit, axis=0, keepdims=True)
    small[5:6, :] = jnp.sum(cot, axis=0, keepdims=True)
    total = grad
    for chunk in range(CHUNKS):
        low = (nt(sent[:, FF_HALF:], down_weight[chunk]) * slope[chunk]).astype(BF16)
        up_grad[chunk] = low
        target = (up_theirs, up_mine)[chunk // half]
        copies.start(up_grad.at[chunk], target.at[:, pl.ds(chunk % half * CHUNK, CHUNK)])
        up_bias_grad[:, pl.ds(places[chunk], CHUNK)] = jnp.sum(
            low.astype(F32), axis=0, keepdims=True
        )
        total = total + nt(low, up_weight[chunk])
    unit = unit_rows[...]
    grad = norm_back(total, unit, inverse[...], gain_one[...])
    first[...] = grad
    copies.start(first, grad_first)
    branch[...] = grad.astype(BF16)
    mine = pl.multiple_of(pos[0] * HALF, HALF)
    theirs = pl.multiple_of((1 - pos[0]) * HALF, HALF)
    copies.start(branch.at[:, pl.ds(mine, HALF)], branch_mine)
    copies.start(branch.at[:, pl.ds(theirs, HALF)], branch_theirs)
    copies.wait(load_out)
    attended[...] = nt(branch[...], out_weight[...]).astype(BF16)
    copies.start(attended, grad_attended)
    small[0:1, :] = jnp.sum(branch[...].astype(F32), axis=0, keepdims=True)
    small[1:2, :] = jnp.sum(total * unit, axis=0, keepdims=True)
    small[2:3, :] = jnp.sum(total, axis=0, keepdims=True)
    copies.finish()


def feed(
    pos,
    keep,
    scaled,
    inverse,
    gain_one,
    shift_one,
    w_out,
    w_up,
    up_bias,
    w_down,
    down_bias,
    gain_two,
    shift_two,
    cot_own,
    cot_other,
):
    items = cot_own.shape[0]
    count = items * 2 * SLOTS
    shape = (count, WIDTH)
    anywhere = pl.BlockSpec(memory_space=pl.ANY)
    near = lambda a: (a, whole(a.shape))
    rows = whole(cot_own.shape)
    return run(
        functools.partial(feed_body, items),
        "feed",
        pos,
        (1,),
        [
            (keep, anywhere),
            (scaled, anywhere),
            near(inverse),
            near(gain_one),
            near(shift_one),
            (w_out, anywhere),
            (w_up, anywhere),
            near(up_bias),
            (w_down, anywhere),
            near(down_bias),
            near(gain_two),
            near(shift_two),
            near(cot_own),
            near(cot_other),
        ],
        [
            ((count, FF_HALF), BF16, anywhere),
            ((count, FF_HALF + WIDTH), BF16, anywhere),
            (cot_own.shape, BF16, rows),
            (cot_own.shape, BF16, rows),
            ((count, FF_HALF), BF16, anywhere),
            ((count, FF_HALF), BF16, anywhere),
            ((1, FF), F32, whole((1, FF))),
            (shape, F32, anywhere),
            ((count, HALF), BF16, anywhere),
            ((count, HALF), BF16, anywhere),
            (shape, BF16, anywhere),
            ((8, WIDTH), F32, whole((8, WIDTH))),
        ],
        scratch=[
            pltpu.VMEM(shape, BF16),
            pltpu.VMEM(shape, F32),
            pltpu.VMEM((WIDTH, WIDTH), BF16),
            pltpu.VMEM((CHUNKS, WIDTH, CHUNK), BF16),
            pltpu.VMEM((CHUNKS, CHUNK, WIDTH), BF16),
            pltpu.VMEM((CHUNKS, count, CHUNK), F32),
            pltpu.VMEM((count, FF_HALF + WIDTH), BF16),
            pltpu.VMEM((count, FF_HALF), BF16),
            pltpu.VMEM((CHUNKS, count, CHUNK), BF16),
            pltpu.VMEM(shape, F32),
            pltpu.VMEM(shape, BF16),
            pltpu.VMEM(shape, BF16),
            pltpu.SemaphoreType.DMA((FEED_COPIES,)),
        ],
        us=20,
        mib=FEED_MIB,
    )


def keep_rows(which, count, cols, place):
    return pl.BlockSpec((None, count, cols), lambda j, pos: (which, 0, place(j, pos)))


def attend_back_half(
    items, mask, ones, queries, keys, values, grad_attended, w_q, w_k, w_v, joined
):
    span = 2 * SLOTS
    upper = lane_half((span, PAIR))
    for item in range(items):
        at = slice(item * span, (item + 1) * span)
        for pair in range(HALF // PAIR):
            cols = slice(pair * PAIR, (pair + 1) * PAIR)
            query = queries[at, cols] * jnp.asarray(SCALE, BF16)
            key = keys[at, cols]
            value = values[at, cols]
            grad_out = grad_attended[at, cols]
            none = jnp.zeros_like(grad_out)
            grads = []
            for head in range(2):
                query_h, key_h = head_operands(
                    upper, head, query, key, ones[...], mask[item]
                )
                probs = softmax_over_keys(nt(key_h, query_h))
                if head == 0:
                    grad_h = jnp.where(upper, none, grad_out)
                else:
                    grad_h = jnp.where(upper, grad_out, none)
                grad_probs = nt(value, grad_h)
                inner = jnp.sum(probs * grad_probs, axis=0, keepdims=True)
                grad_scores = (probs * (grad_probs - inner)).astype(BF16)
                grads.append(
                    (
                        tn(grad_scores, key) * SCALE,
                        nn(grad_scores, query),
                        nn(probs.astype(BF16), grad_out),
                    )
                )
            for index in range(3):
                place = slice(index * HALF + pair * PAIR, index * HALF + (pair + 1) * PAIR)
                joined[at, place] = jnp.where(
                    upper, grads[1][index], grads[0][index]
                ).astype(BF16)
    parts = [joined[:, index * HALF : (index + 1) * HALF] for index in range(3)]
    sums = [jnp.sum(parts[index].astype(F32), axis=0, keepdims=True) for index in (0, 2)]
    total = nt(parts[0], w_q[...]) + nt(parts[1], w_k[...]) + nt(parts[2], w_v[...])
    return total, sums


def attend_back_body(items, pos, *refs):
    *ins, first, second, grad_first, small_in, up_bias, theirs, mine, own, other, small, total, joined = refs
    step = pl.program_id(0)
    span = 2 * SLOTS
    part, sums = attend_back_half(items, *ins, joined)

    @pl.when(step == 0)
    def _():
        theirs[:, : 3 * HALF] = joined[...]
        theirs[:, 3 * HALF :] = first[...]
        total[...] = grad_first[...] + part
        small[...] = jnp.zeros_like(small)
        small[0:8, :] = small_in[...]
        for index in range(FF // WIDTH):
            small[6 + index : 7 + index, :] = up_bias[:, index * WIDTH : (index + 1) * WIDTH]

    @pl.when(step == 1)
    def _():
        mine[:, : 3 * HALF] = joined[...]
        mine[:, 3 * HALF :] = second[...]
        for item in range(items):
            at = slice(item * span, item * span + SLOTS)
            own[item] = total[at, :] + part[at]
            at = slice(item * span + SLOTS, (item + 1) * span)
            other[item] = (total[at, :] + part[at]).astype(BF16)

    place = pl.multiple_of(lax.rem(step + 1 + pos[0], 2) * HALF, HALF)
    for index in range(2):
        small[10 + index : 11 + index, pl.ds(place, HALF)] = sums[index]


def attend_back(
    pos, mask, ones, queries, keys, values, grad_attended, w_qkv, first, second, grad_first, small, up_bias, after
):
    count = queries.shape[0]
    items = mask.shape[0]
    half = lambda j, pos: lax.rem(j + 1 + pos[0], 2)
    flat = pl.BlockSpec((count, HALF), lambda j, pos: (0, half(j, pos)))
    weight = lambda k: pl.BlockSpec((WIDTH, HALF), lambda j, pos: (0, 2 * k + half(j, pos)))
    joined = ((count, 4 * HALF), BF16, whole((count, 4 * HALF)))
    rows = whole((items, SLOTS, WIDTH))
    return run(
        functools.partial(attend_back_body, items),
        "attend_back",
        pos,
        (2,),
        [
            (mask, whole(mask.shape)),
            (ones, whole(ones.shape)),
            (queries, flat),
            (keys, flat),
            (values, flat),
            (grad_attended, flat),
            (w_qkv, weight(0)),
            (w_qkv, weight(1)),
            (w_qkv, weight(2)),
        ]
        + [(a, whole(a.shape)) for a in (first, second, grad_first, small, up_bias)],
        [
            joined,
            joined,
            ((items, SLOTS, WIDTH), F32, rows),
            ((items, SLOTS, WIDTH), BF16, rows),
            ((16, WIDTH), F32, whole((16, WIDTH))),
        ],
        after=after,
        scratch=[pltpu.VMEM((count, WIDTH), F32), pltpu.VMEM((count, 3 * HALF), BF16)],
        us=0.6,
        mib=32,
    )


TALL = HALF
LOW = TALL // 2
FAR, ACROSS, ALONG, OWN = 3, 2, 1, 0
PIECE = (TALL, WIDTH)


def quarter(pos, there):
    return pos[1] ^ (there >> 1), pos[2] ^ (there & 1)


def order_of(kind, step):
    first, second = (ACROSS, ALONG) if kind == "up" else (ALONG, ACROSS)
    return jnp.where(step == 0, FAR, jnp.where(step == 1, first, jnp.where(step == 2, second, OWN)))


def gradient_body(kind, block, outs, pos, *refs):
    ins, outs = refs[:-outs], refs[-outs:]
    step = pl.program_id(0)
    value = block(quarter(pos, order_of(kind, step))[1], *ins).astype(BF16)
    if kind == "mixed":
        targets = [None, outs[2], outs[3], outs[4]]
    else:
        targets = [outs[0].at[0], outs[0].at[1], outs[1], outs[2]]
    for index, target in enumerate(targets):

        @pl.when(step == index)
        def _(target=target):
            if target is None:
                outs[0][...] = value[:LOW]
                outs[1][...] = value[LOW:]
            else:
                target[...] = value


def plain_block(along, left_a, left_b, right_a, right_b):
    return tn(left_a[...], right_a[...]) + tn(left_b[...], right_b[...])


def mixed_block(along, rows_a, rows_b, att_a, att_b, right_a, right_b):
    left_a = jnp.where(along == 0, rows_a[...], att_a[...])
    left_b = jnp.where(along == 0, rows_b[...], att_b[...])
    return jnp.concatenate(
        [
            tn(rows_a[...], right_a[:, :HALF]) + tn(rows_b[...], right_b[:, :HALF]),
            tn(left_a, right_a[:, HALF:]) + tn(left_b, right_b[:, HALF:]),
        ],
        axis=1,
    )


def gradient(kind, pos, operands, after):
    count = operands[-1].shape[0]
    across = lambda j, pos: quarter(pos, order_of(kind, j))[0]
    along = lambda j, pos: quarter(pos, order_of(kind, j))[1]
    block = plain_block
    if kind == "down":
        lefts = pl.BlockSpec(
            (count, TALL), lambda j, pos: (0, 2 * across(j, pos) + along(j, pos))
        )
        rights = pl.BlockSpec((count, WIDTH), lambda j, pos: (0, FF_HALF // WIDTH))
        specs = [lefts, lefts, rights, rights]
    else:
        rights = pl.BlockSpec((count, WIDTH), lambda j, pos: (0, along(j, pos)))
        if kind == "up":
            lefts = keep_rows(2, count, TALL, across)
            specs = [lefts, lefts, rights, rights]
        else:
            rows, att = keep_rows(0, count, TALL, across), keep_rows(1, count, TALL, across)
            specs = [rows, rows, att, att, rights, rights]
            block = mixed_block
    if kind == "mixed":
        shapes = [(LOW, WIDTH)] * 2 + [PIECE] * 3
    else:
        shapes = [(2,) + PIECE] + [PIECE] * 2
    return run(
        functools.partial(gradient_body, kind, block, len(shapes)),
        kind + "_gradient",
        pos,
        (4,),
        list(zip(operands, specs)),
        [(shape, BF16, whole(shape)) for shape in shapes],
        after=after,
        us=0.3,
        mib=20,
    )


def sum_body(share, pos, *refs):
    ins = refs[:-3] if share else refs[:-1]
    total = ins[0][...].astype(F32)
    for ref in ins[1:]:
        total = total + ref[...].astype(F32)
    if not share:
        refs[-1][...] = total.astype(BF16)
        return
    held = refs[-1]
    held[...] = total
    for turn in range(2):
        first = pl.multiple_of((pos[3] ^ turn) * LOW, LOW)
        refs[turn - 3][...] = held[pl.ds(first, LOW), :].astype(BF16)


def sum_of(pos, arrays, after, share=False, carry=(), us=1):
    shape = arrays[0].shape
    item = lambda index: pl.BlockSpec((None,) + PIECE, lambda *_: (index, 0, 0))
    shapes = [(LOW, WIDTH)] * 2 if share else [shape]
    out, *more = run(
        functools.partial(sum_body, share),
        "sum_shares" if share else "sum_of",
        pos,
        (1,),
        [
            (a[0], item(a[1])) if isinstance(a, tuple) else (a, whole(shape))
            for a in arrays
        ],
        [(shape, BF16, whole(shape)) for shape in shapes],
        after=after,
        scratch=[pltpu.VMEM(shape, F32)] if share else [],
        us=us,
        mib=8,
        carry=carry,
    )
    return (out if share else out[0]), *more


def sides_body(pos, along, across, low, high, along_out, across_out):
    along_out[:LOW, :] = along[:LOW, :]
    along_out[LOW:, :] = (along[LOW:, :].astype(F32) + high[...].astype(F32)).astype(BF16)
    across_out[:LOW, :] = (across[:LOW, :].astype(F32) + low[...].astype(F32)).astype(BF16)
    across_out[LOW:, :] = across[LOW:, :]


def sum_sides(pos, along, across, low, high, after, carry=()):
    return run(
        sides_body,
        "sum_sides",
        pos,
        (1,),
        [(a, whole(a.shape)) for a in (along, across, low, high)],
        [(PIECE, BF16, whole(PIECE))] * 2,
        after=after,
        carry=carry,
        us=0.1,
        mib=8,
    )


def split_body(pos, own, first, second, low, high, packed):
    low[...] = first[:LOW, :]
    high[...] = second[LOW:, :]
    for index, ref in enumerate((own, first, second)):
        packed[index] = ref[...]


def split(pos, own, first, second, after):
    half = (LOW, WIDTH)
    return run(
        split_body,
        "split",
        pos,
        (1,),
        [(a, whole(PIECE)) for a in (own, first, second)],
        [(half, BF16, whole(half))] * 2 + [((3,) + PIECE, BF16, whole((3,) + PIECE))],
        after=after,
        us=1,
        mib=10,
    )


def pack_body(pos, *refs):
    for index, ref in enumerate(refs[:-1]):
        refs[-1][index] = ref[...]


def pack(pos, pieces, after):
    shape = (len(pieces),) + PIECE
    out, token = run(
        pack_body,
        "pack",
        pos,
        (1,),
        [(a, whole(PIECE)) for a in pieces],
        [(shape, BF16, whole(shape))],
        after=after,
        us=0.1,
        mib=12,
    )
    return out[0], token


def stack_halves(pos, low, high, after):
    half = (LOW, WIDTH)
    out, token = run(
        pack_body,
        "stack_halves",
        pos,
        (1,),
        [(low, whole(half)), (high, whole(half))],
        [((2,) + half, BF16, whole((2,) + half))],
        after=after,
        us=0.1,
        mib=6,
    )
    return out[0], token


def join_body(pos, mine, theirs, out):
    for turn, ref in enumerate((mine, theirs)):
        first = pl.multiple_of((pos[3] ^ turn) * LOW, LOW)
        out[pl.ds(first, LOW), :] = ref[...]


def join_shares(pos, shares, after, carry=()):
    out, *more = run(
        join_body,
        "join_shares",
        pos,
        (1,),
        [(a, whole(a.shape)) for a in shares],
        [(PIECE, BF16, whole(PIECE))],
        after=after,
        us=0.1,
        mib=6,
        carry=carry,
    )
    return out[0], *more


def place_body(kind, entries, outs, pos, *refs):
    sources = iter(refs)
    pieces = []
    for _, _, _, _, index in entries:
        if not index:
            ref = next(sources)
        pieces.append(ref if index is None else ref.at[index])
    targets = refs[len(refs) - 4 - outs : len(refs) - 4]
    taken, given, in_sems, out_sems = refs[-4:]
    fetches = []
    for index, (rows, *_) in enumerate(entries):
        fetch = pltpu.make_async_copy(
            pieces[index], taken.at[index, pl.ds(0, rows)], in_sems.at[index]
        )
        fetch.start()
        fetches.append(fetch)

    def sends(index):
        rows, theirs, there, start, _ = entries[index]
        half = pos[0] ^ theirs
        across, along = quarter(pos, there)
        source = given.at[index]
        if kind == "down":
            first = pl.multiple_of((4 * half + 2 * across + along) * TALL + start, LOW)
            yield None, source.at[pl.ds(0, rows)], targets[0].at[pl.ds(first, rows)], 0
            return
        first = pl.multiple_of(across * TALL + start, LOW)
        if kind == "up":
            column = pl.multiple_of((2 * half + along) * WIDTH, WIDTH)
            target = targets[0].at[pl.ds(first, rows), pl.ds(column, WIDTH)]
            yield None, source.at[pl.ds(0, rows)], target, 0
            return
        for part in range(2):
            source_part = source.at[pl.ds(0, rows), pl.ds(part * HALF, HALF)]
            column = pl.multiple_of(jnp.minimum(2 * along + part, 2) * WIDTH + half * HALF, HALF)
            target = targets[0].at[pl.ds(first, rows), pl.ds(column, HALF)]
            if part == 0:
                yield None, source_part, target, 0
            else:
                yield along == 0, source_part, target, 1
                column = pl.multiple_of(half * HALF, HALF)
                target = targets[1].at[pl.ds(first, rows), pl.ds(column, HALF)]
                yield along == 1, source_part, target, 1

    def each(index, act):
        for condition, source, target, sem in sends(index):
            copy = pltpu.make_async_copy(source, target, out_sems.at[index, sem])
            if condition is None:
                act(copy)
            else:

                @pl.when(condition)
                def _(copy=copy):
                    act(copy)

    for index, (rows, *_) in enumerate(entries):
        fetches[index].wait()
        given[index, :rows, :] = taken[index, :rows, :].astype(F32)
        each(index, lambda copy: copy.start())
    for index in range(len(entries)):
        each(index, lambda copy: copy.wait())


def place(kind, pos, pieces, before, after):
    pieces = [piece if len(piece) == 5 else piece + (None,) for piece in pieces]
    entries = tuple((p.shape[-2],) + tuple(more) for p, *more in pieces)
    shapes = {
        "down": [(FF, WIDTH)],
        "up": [(WIDTH, FF)],
        "mixed": [(WIDTH, 3 * WIDTH), (WIDTH, WIDTH)],
    }[kind]
    anywhere = pl.BlockSpec(memory_space=pl.ANY)
    arrays = [p for p, *_, index in pieces if not index]
    ins = [(a, anywhere) for a in arrays + list(before)]
    count = len(entries)
    return run(
        functools.partial(place_body, kind, entries, len(shapes)),
        "place_" + kind,
        pos,
        (1,),
        ins,
        [(shape, F32, anywhere) for shape in shapes],
        after=after,
        scratch=[
            pltpu.VMEM((count, TALL, WIDTH), BF16),
            pltpu.VMEM((count, TALL, WIDTH), F32),
            pltpu.SemaphoreType.DMA((count,)),
            pltpu.SemaphoreType.DMA((count, 2)),
        ],
        aliases={1 + len(arrays) + index: index for index in range(len(before))},
        us=0.02,
        mib=22,
    )


def place_rows_body(pos, own, got, own_grad, got_grad, out, grad):
    @pl.when(pl.program_id(0) == 0)
    def _():
        out[...] = own[...]
        grad[...] = own_grad[...]

    @pl.when(pl.program_id(0) == 1)
    def _():
        out[...] = got[...]
        grad[...] = got_grad[...].astype(F32)


def place_rows(pos, own, got, own_grad, got_grad, after):
    items = own.shape[0]
    spec = pl.BlockSpec(own.shape, lambda step, pos: (pos[1] ^ step, 0, 0))
    shape = (2 * items,) + own.shape[1:]
    return run(
        place_rows_body,
        "place_rows",
        pos,
        (2,),
        [(a, whole(own.shape)) for a in (own, got, own_grad, got_grad)],
        [(shape, BF16, spec), (shape, F32, spec)],
        after=after,
        us=0.02,
        mib=10,
    )


def local(
    batch,
    tokens,
    caption_lengths,
    region_mask,
    w_qkv,
    query_bias,
    value_bias,
    w_out,
    out_bias,
    w_up,
    up_bias,
    w_down,
    down_bias,
    gain_one,
    shift_one,
    gain_two,
    shift_two,
    cotangent,
):
    swap_core = [(i, i ^ 1) for i in range(batch)]
    swap_along = [(i, i ^ 2) for i in range(batch)]
    swap_across = [(0, 1), (1, 0)]
    line = [[4 * k + i for k in range(batch // 4)] for i in range(4)]
    same_core = [[2 * k + i for k in range(batch // 2)] for i in range(2)]
    core = lambda a: lax.ppermute(a, "batch", swap_core)
    along = lambda a: lax.ppermute(a, "batch", swap_along)
    across = lambda a: lax.ppermute(a, "mod", swap_across)

    place_y = lax.axis_index("mod")
    place_b = lax.axis_index("batch")
    pos = jnp.stack([place_b % 2, place_y, (place_b // 2) % 2, (place_b // 4) % 2]).astype(jnp.int32)
    items = tokens.shape[0] // 2
    mine = place_y * items
    rest = (1 - place_y) * items
    rows = lambda a, start: lax.dynamic_slice_in_dim(a, start, items, axis=0)

    other_tokens = across(rows(tokens, rest))
    other_cot = across(rows(cotangent, rest))
    own_tokens = rows(tokens, mine)
    own_cot = rows(cotangent, mine)

    slot = lax.broadcasted_iota(jnp.int32, (items, SLOTS), 1)
    text = slot < rows(caption_lengths, mine)[:, None]
    region = rows(region_mask, mine) > 0
    valid = jnp.concatenate(
        [jnp.where(place_y == 0, text, region), jnp.where(place_y == 0, region, text)], axis=1
    )
    lane = lax.broadcasted_iota(jnp.int32, (1, 1, PAIR), 2) % HEAD_DIM == 0
    mask = jnp.where(lane & ~valid[:, :, None], MASKED, 0.0).astype(BF16)
    ones = jnp.where(
        lax.broadcasted_iota(jnp.int32, (2 * SLOTS, PAIR), 1) % HEAD_DIM == 0, 1.0, 0.0
    ).astype(BF16)
    line_of = lambda a: a.reshape(1, -1)

    (queries, keys, values, keep, scaled, inverse), _ = attend(
        pos,
        own_tokens,
        other_tokens,
        mask,
        ones,
        w_qkv,
        line_of(query_bias),
        line_of(value_bias),
        w_out,
        line_of(out_bias),
        line_of(gain_one),
        line_of(shift_one),
    )
    (
        (
            act_mine,
            send,
            out_own,
            out_other,
            up_theirs,
            up_mine,
            up_bias_grad,
            grad_first,
            branch_theirs,
            branch_mine,
            grad_attended,
            small,
        ),
        done,
    ) = feed(
        pos,
        keep,
        scaled,
        inverse,
        line_of(gain_one),
        line_of(shift_one),
        w_out,
        w_up,
        line_of(up_bias),
        w_down,
        line_of(down_bias),
        line_of(gain_two),
        line_of(shift_two),
        own_cot,
        other_cot,
    )
    send_got, keep_got, up_got = core(send), core(keep), core(up_theirs)
    out_got = across(out_other)
    by_shares = batch == 16
    near = lambda a: lax.ppermute(a, "batch", [(i, i ^ 4) for i in range(batch)])
    wide = lambda a: lax.ppermute(a, "batch", [(i, i ^ 8) for i in range(batch)])

    def line_sum(piece, turn):
        return lax.psum(piece, "batch", axis_index_groups=line[turn:] + line[:turn])

    hops = [across]
    bit = 2
    while bit < batch:
        hops.append(
            lambda a, bit=bit: lax.ppermute(a, "batch", [(i, i ^ bit) for i in range(batch)])
        )
        bit *= 2
    hops.append(core)

    def ride(kernel, *args, **more):
        nonlocal small, got, riding
        if not riding:
            return kernel(*args, **more)
        out, done, small = kernel(
            *args, **more, carry=(small,) if got is None else (small, got)
        )
        got = hops.pop(0)(small) if hops else None
        return out, done

    (down_pair, down_across, down_own), done = gradient(
        "down", pos, (act_mine, send_got, send, send_got), (done,)
    )
    down_pair = along(down_pair)
    (up_pair, up_along, up_own), done = gradient(
        "up", pos, (keep, keep_got, up_mine, up_got), (done, out_got)
    )
    up_pair = across(up_pair)
    (joint_theirs, joint_mine, grad_own, grad_other, small), done = attend_back(
        pos,
        mask,
        ones,
        queries,
        keys,
        values,
        grad_attended,
        w_qkv,
        branch_theirs,
        branch_mine,
        grad_first,
        small,
        up_bias_grad,
        (done,),
    )
    joint_got = core(joint_theirs)
    down_across, done = sum_of(pos, (down_across, (down_pair, 0)), (done,))
    down_across = across(down_across)
    up_along, done = sum_of(pos, (up_along, (up_pair, 0)), (done,))
    up_along = along(up_along)
    (mixed_low, mixed_high, mixed_along, mixed_across, mixed_own), done = gradient(
        "mixed", pos, (keep, keep_got, keep, keep_got, joint_mine, joint_got), (done,)
    )
    mixed_low, mixed_high = along(mixed_low), across(mixed_high)
    got, riding = None, False

    def halves(arrays, done, turn):
        parts, done = ride(sum_of, pos, arrays, (done,), share=by_shares, us=0.1)
        if by_shares:
            return (parts[0], near(parts[1])), done
        return line_sum(parts, turn), done

    def widen(parts, after):
        if not by_shares:
            return parts, after[0]
        half, done = ride(sum_of, pos, parts, after, us=0.1)
        return (half, wide(half)), done

    def narrow(parts, after):
        if not by_shares:
            return parts, after[0]
        half, done = ride(sum_of, pos, parts, after, us=0.1)
        return (half, near(half)), done

    def joined(parts, after):
        return ride(join_shares, pos, parts, after) if by_shares else (parts, after[0])

    down_sum, done = halves((down_own, (down_pair, 1), down_across), done, 0)
    up_sum, done = halves((up_own, (up_pair, 1), up_along), done, 1)
    (mixed_along, mixed_across), done = ride(
        sum_sides, pos, mixed_along, mixed_across, mixed_low, mixed_high, (done,)
    )
    mixed_along, mixed_across = along(mixed_along), across(mixed_across)
    down_sum, done = widen(down_sum, (done,))
    riding = True
    down_sum, done = narrow(down_sum, (done,))
    up_sum, done = widen(up_sum, (done,))
    mixed_sum, done = halves((mixed_own, mixed_along, mixed_across), done, 2)
    grad_got = across(grad_other)
    down_sum, done = joined(down_sum, (done, grad_got))
    down_x, down_y = along(down_sum), across(down_sum)
    up_sum, done = narrow(up_sum, (done,))
    mixed_sum, done = widen(mixed_sum, (done, down_x, down_y))
    (layer_output, input_grad), done = place_rows(
        pos, out_own, out_got, grad_own, grad_got, (done,)
    )
    up_sum, done = joined(up_sum, (done,))
    up_x, up_y = along(up_sum), across(up_sum)
    mixed_sum, done = narrow(mixed_sum, (done, up_x, up_y))
    while hops or got is not None:
        small = small + (hops.pop(0)(small) if got is None else got)
        got = None
    vectors = [small[index] for index in range(12)]
    vectors[6] = small[6:10].reshape(FF)
    seen = tuple(vectors[index] for index in (0, 1, 2, 3, 4, 5, 6, 10, 11))
    down_pack, done = pack(pos, (down_sum, down_x, down_y, across(down_x)), (done,))
    mixed_sum, done = joined(mixed_sum, (done,))
    mixed_x, mixed_y = along(mixed_sum), across(mixed_sum)
    up_pack, done = pack(pos, (up_sum, up_x, up_y, along(up_y)), (done,))
    def both(pieces):
        return [(p, 0, there, start) for p, there, start in pieces] + [
            (core(p), 1, there, start) for p, there, start in pieces
        ]

    def packed(pieces):
        places = list(enumerate((OWN, ALONG, ACROSS, FAR)))[: pieces.shape[0]]
        return [
            (array, theirs, there, 0, index)
            for theirs, array in enumerate((pieces, core(pieces)))
            for index, there in places
        ]

    (grad_down,), done = place(
        "down",
        pos,
        packed(down_pack),
        (),
        (done,),
    )
    (grad_up,), done = place(
        "up",
        pos,
        packed(up_pack),
        (),
        (done,),
    )
    (mixed_low, mixed_high, mixed_pack), done = split(pos, mixed_sum, mixed_x, mixed_y, (done,))
    mixed_low, mixed_high = across(mixed_low), along(mixed_high)
    partial, done = place(
        "mixed",
        pos,
        packed(mixed_pack),
        (),
        (done,),
    )
    last, done = stack_halves(pos, mixed_low, mixed_high, (done,) + seen)
    ends = [
        (array, theirs, FAR, start, index)
        for theirs, array in enumerate((last, core(last)))
        for index, start in enumerate((0, LOW))
    ]
    (grad_qkv, grad_out), done = place("mixed", pos, ends, partial, (done,))
    return (
        layer_output,
        input_grad,
        grad_qkv,
        vectors[10],
        vectors[11],
        grad_out,
        vectors[0],
        grad_up,
        vectors[6],
        grad_down,
        vectors[3],
        vectors[1],
        vectors[2],
        vectors[4],
        vectors[5],
    )


def solution(mesh):
    rows = P("batch", "mod", None)
    return jax.shard_map(
        functools.partial(local, mesh.shape["batch"]),
        mesh=mesh,
        in_specs=(rows, P("batch"), P("batch", None)) + (P(),) * 13 + (rows,),
        out_specs=(rows, rows) + (P(),) * 13,
        check_vma=False,
    )
```
